128 devices in a mesh: dp: 8 (over y, core), ctx: 2 (over x_hi), fsdp: 8 (over x_lo, z).
Axes of the slice: x: 4 (x_hi: 2, x_lo: 2; x = x_hi * 2 + x_lo), y: 4, z: 4, core: 2. Of those that a mesh axis runs over, the one named last changes fastest.
Arguments:
- tokens: bfloat16 [8, 2048, 1536], P('dp', ('fsdp', 'ctx')), may hold values from -6 to 6
- lengths: int32 [8], P('dp'), may hold values from 1024 to 2048, as said below
- cotangent: bfloat16 [8, 2048, 1536], P('dp', ('fsdp', 'ctx')), may hold values from -6 to 6
- attend_gain: float32 [1536], replicated, may hold values from 0.5 to 1.5
- query_weight: bfloat16 [1536, 1536], P(('ctx', 'fsdp')), may hold values from -0.21875 to 0.21875
- keyval_weight: bfloat16 [1536, 256], P(('ctx', 'fsdp')), may hold values from -0.15625 to 0.15625
- attend_output: bfloat16 [1536, 1536], P(('ctx', 'fsdp')), may hold values from -1.75 to 1.75
- lower_gain: float32 [1536], replicated, may hold values from 0.5 to 1.5
- lower_gate: bfloat16 [1536, 4608], P(('ctx', 'fsdp')), may hold values from -0.15625 to 0.15625
- lower_lift: bfloat16 [1536, 4608], P(('ctx', 'fsdp')), may hold values from -0.15625 to 0.15625
- lower_drop: bfloat16 [4608, 1536], P(('ctx', 'fsdp')), may hold values from -0.09375 to 0.09375
- recur_gain: float32 [1536], replicated, may hold values from 0.5 to 1.5
- recur_input: bfloat16 [1536, 2048], P(('ctx', 'fsdp')), may hold values from -0.15625 to 0.15625
- recur_branch: bfloat16 [1536, 2048], P(('ctx', 'fsdp')), may hold values from -0.15625 to 0.15625
- recur_output: bfloat16 [2048, 1536], P(('ctx', 'fsdp')), may hold values from -0.375 to 0.375
- temporal_kernel: float32 [4, 2048], replicated, may hold values from -3 to 3
- decay_gate: bfloat16 [16, 128, 128], replicated, may hold values from -2 to 2
- input_gate: bfloat16 [16, 128, 128], replicated, may hold values from -0.5 to 0.5
- decay_rate: float32 [2048], replicated, as said below
- upper_gain: float32 [1536], replicated, may hold values from 0.5 to 1.5
- upper_gate: bfloat16 [1536, 4608], P(('ctx', 'fsdp')), may hold values from -0.15625 to 0.15625
- upper_lift: bfloat16 [1536, 4608], P(('ctx', 'fsdp')), may hold values from -0.15625 to 0.15625
- upper_drop: bfloat16 [4608, 1536], P(('ctx', 'fsdp')), may hold values from -0.09375 to 0.09375
Outputs:
- out_tokens: bfloat16 [8, 2048, 1536], P('dp', ('fsdp', 'ctx'))
- grad_tokens: float32 [8, 2048, 1536], P('dp', ('fsdp', 'ctx'))
- grad_attend_gain: float32 [1536], replicated
- grad_query_weight: float32 [1536, 1536], P(('ctx', 'fsdp'))
- grad_keyval_weight: float32 [1536, 256], P(('ctx', 'fsdp'))
- grad_attend_output: float32 [1536, 1536], P(('ctx', 'fsdp'))
- grad_lower_gain: float32 [1536], replicated
- grad_lower_gate: float32 [1536, 4608], P(('ctx', 'fsdp'))
- grad_lower_lift: float32 [1536, 4608], P(('ctx', 'fsdp'))
- grad_lower_drop: float32 [4608, 1536], P(('ctx', 'fsdp'))
- grad_recur_gain: float32 [1536], replicated
- grad_recur_input: float32 [1536, 2048], P(('ctx', 'fsdp'))
- grad_recur_branch: float32 [1536, 2048], P(('ctx', 'fsdp'))
- grad_recur_output: float32 [2048, 1536], P(('ctx', 'fsdp'))
- grad_temporal_kernel: float32 [4, 2048], replicated
- grad_decay_gate: float32 [16, 128, 128], replicated
- grad_input_gate: float32 [16, 128, 128], replicated
- grad_decay_rate: float32 [2048], replicated
- grad_upper_gain: float32 [1536], replicated
- grad_upper_gate: float32 [1536, 4608], P(('ctx', 'fsdp'))
- grad_upper_lift: float32 [1536, 4608], P(('ctx', 'fsdp'))
- grad_upper_drop: float32 [4608, 1536], P(('ctx', 'fsdp'))
The draws below stay inside these ranges and needn't reach their ends.
Inputs may be any that keep to these rules, and one draw needn't show every extreme that they name: `lengths`: valid slots of a sequence form a prefix of its slots. `decay_rate`: one decay parameter for each recurrence channel.
All inputs are finite; a program needn't handle non-finite values.
Results may differ from the reference program's by a relative error of at most 0.028.
Values may be sent and summed in bfloat16 or wider, within the bound.
No kernel may reach another device: no remote copies, remote signals or barrier semaphores. Data moves between devices by JAX's collectives and lax.ppermute only.
A program may use at most 384 MiB of HBM per device.

```python
import math
import jax
import jax.numpy as jnp
from jax import lax

D = 1536
HEADS = 12
HD = 128
FF = 4608
RW = 2048
RB = 128
CONV = 4
WINDOW = 1024
SLOTS = 2048
SEQS = 8
N_CTX = 2
N_FSDP = 8


def draw_lengths(key, part):
    key = jax.random.fold_in(key, 11)
    first_key, second_key, third_key = jax.random.split(key, 3)
    spread = jax.random.randint(first_key, (SEQS,), SLOTS // 2, SLOTS + 1, dtype=jnp.int32)
    longest = jax.random.randint(second_key, (), 0, SEQS, dtype=jnp.int32)
    shortest = (longest + 1 + jax.random.randint(third_key, (), 0, SEQS - 1, dtype=jnp.int32)) % SEQS
    position = jnp.arange(SEQS, dtype=jnp.int32)
    spread = jnp.where(position == longest, SLOTS, spread)
    return jnp.where(position == shortest, SLOTS // 2, spread).astype(jnp.int32)


def draw_decay_rate(key, part):
    key = jax.random.fold_in(key, 23)
    lower_end = math.log(0.05 / SLOTS)
    upper_end = math.log(1.0 / 30.0)
    rates = jnp.exp(jax.random.uniform(key, (RW,), jnp.float32, lower_end, upper_end))
    return jnp.log(jnp.expm1(rates / 6.0))


def level_of(own_key, extent, cuts, least, largest):
    def one(axis_at, parts):
        steps = jax.random.uniform(jax.random.fold_in(jax.random.fold_in(own_key, 6), axis_at), (parts,), jnp.float32, least / len(cuts), largest / len(cuts))
        return jnp.repeat(jnp.exp(steps), extent[axis_at] // parts).reshape((-1,) + (1,) * (len(extent) - axis_at - 1))

    level = one(*cuts[0])
    for cut in cuts[1:]:
        level = level * one(*cut)
    return level


def normal_values(key, shape, scale, reach, pieces=(), kind=jnp.bfloat16):
    entries = scale * jax.random.normal(key, shape, jnp.float32)
    if pieces:
        entries = entries * level_of(key, shape, pieces, -0.22, 0.18)
    return jnp.clip(entries, -reach, reach).astype(kind)


def setup_inputs(seed: int = 0) -> dict:
    key_list = jax.random.split(jax.random.key(seed), 24)
    tokens = normal_values(key_list[0], (SEQS, SLOTS, D), 1.0, 6.0, ((0, 8), (1, 16)))
    lengths = draw_lengths(jax.random.fold_in(key_list[23], 71), 0)
    cotangent = normal_values(key_list[2], (SEQS, SLOTS, D), 1.0, 6.0, ((0, 8), (1, 16)))
    attend_gain = jnp.clip(1.0 + 0.1 * jax.random.normal(key_list[3], (D,), jnp.float32), 0.5, 1.5)
    query_weight = normal_values(key_list[4], (D, HEADS * HD), (D // 2) ** -0.5, 0.21875, ((0, 16),))
    keyval_weight = normal_values(key_list[5], (D, 2 * HD), D ** -0.5, 0.15625, ((0, 16),))
    attend_output = normal_values(key_list[6], (HEADS * HD, D), (max(HEADS * HD * 8 // WINDOW, 1)) ** -0.5, 1.75, ((0, 16),))
    lower_gain = jnp.clip(1.0 + 0.1 * jax.random.normal(key_list[7], (D,), jnp.float32), 0.5, 1.5)
    lower_gate = normal_values(key_list[8], (D, FF), D ** -0.5, 0.15625, ((0, 16),))
    lower_lift = normal_values(key_list[9], (D, FF), D ** -0.5, 0.15625, ((0, 16),))
    lower_drop = normal_values(key_list[10], (FF, D), FF ** -0.5, 0.09375, ((0, 16),))
    recur_gain = jnp.clip(1.0 + 0.1 * jax.random.normal(key_list[11], (D,), jnp.float32), 0.5, 1.5)
    recur_input = normal_values(key_list[12], (D, RW), D ** -0.5, 0.15625, ((0, 16),))
    recur_branch = normal_values(key_list[13], (D, RW), D ** -0.5, 0.15625, ((0, 16),))
    recur_output = normal_values(key_list[14], (RW, D), (RW // 8) ** -0.5, 0.375, ((0, 16),))
    temporal_kernel = normal_values(key_list[15], (CONV, RW), CONV ** -0.5, 3.0, (), jnp.float32)
    decay_gate = normal_values(key_list[16], (RW // RB, RB, RB), (max(RB // 16, 1)) ** -0.5, 2.0)
    input_gate = normal_values(key_list[17], (RW // RB, RB, RB), RB ** -0.5, 0.5)
    decay_rate = draw_decay_rate(jax.random.fold_in(key_list[23], 71), 0)
    upper_gain = jnp.clip(1.0 + 0.1 * jax.random.normal(key_list[19], (D,), jnp.float32), 0.5, 1.5)
    upper_gate = normal_values(key_list[20], (D, FF), D ** -0.5, 0.15625, ((0, 16),))
    upper_lift = normal_values(key_list[21], (D, FF), D ** -0.5, 0.15625, ((0, 16),))
    upper_drop = normal_values(key_list[22], (FF, D), FF ** -0.5, 0.09375, ((0, 16),))
    return dict(tokens=tokens, lengths=lengths, cotangent=cotangent, attend_gain=attend_gain, query_weight=query_weight, keyval_weight=keyval_weight, attend_output=attend_output, lower_gain=lower_gain, lower_gate=lower_gate, lower_lift=lower_lift, lower_drop=lower_drop, recur_gain=recur_gain, recur_input=recur_input, recur_branch=recur_branch, recur_output=recur_output, temporal_kernel=temporal_kernel, decay_gate=decay_gate, input_gate=input_gate, decay_rate=decay_rate, upper_gain=upper_gain, upper_gate=upper_gate, upper_lift=upper_lift, upper_drop=upper_drop)


EPSILON = 1e-06
DECAY_SCALE = 8.0

@jax.custom_vjp
def low(v):
    return lax.optimization_barrier(v.astype(jnp.bfloat16)).astype(jnp.float32)

@jax.custom_vjp
def low_back(v):
    return v

def low_keep(v):
    return (low(v), None)

def low_pass(kept, grad):
    return (grad,)

def back_keep(v):
    return (v, None)

def back_low(kept, grad):
    return (low(grad),)
low.defvjp(low_keep, low_pass)
low_back.defvjp(back_keep, back_low)

def product(left, right):
    return jnp.dot(left, right, precision=lax.Precision.HIGHEST)

def normalize(values, gain):
    return values * lax.rsqrt(lax.optimization_barrier(jnp.mean(values * values, axis=-1, keepdims=True)) + EPSILON) * gain

def smooth_gelu(values):
    return jax.nn.gelu(values, approximate=True)

def compose(earlier, later):
    return (earlier[0] * later[0], later[0] * earlier[1] + later[1])

def gate_terms(pre_decay, pre_admit, conv_out, decay_rate):
    retain = jax.nn.sigmoid(pre_decay)
    admit = jax.nn.sigmoid(pre_admit)
    log_decay = -DECAY_SCALE * jax.nn.softplus(decay_rate) * (0.25 + retain)
    return (jnp.exp(log_decay), jnp.sqrt(-jnp.expm1(2.0 * log_decay)) * admit * conv_out)

def attention(normed, query_weight, keyval_weight, attend_output):
    seq_len = normed.shape[0]
    block_rows = seq_len // N_FSDP
    group_heads = HEADS // N_CTX
    lowered = low(normed)
    queries = low_back(low(product(lowered, query_weight)))
    keyvals = low(low_back(product(lowered, keyval_weight)))
    grouped = jnp.stack([low_back(keyvals) for copy_index in range(N_CTX)])
    padded = jnp.concatenate([jnp.zeros((N_CTX, WINDOW, 2 * HD), jnp.float32), grouped], axis=1)

    def one_block(block_index):
        start = block_index * block_rows
        query_rows = lax.dynamic_slice_in_dim(queries, start, block_rows, 0).reshape(block_rows, N_CTX, group_heads, HD)
        key_rows = lax.dynamic_slice_in_dim(padded, start, WINDOW + block_rows, 1)
        scores = jnp.einsum('qchd,ckd->chqk', query_rows, key_rows[:, :, :HD], precision=lax.Precision.HIGHEST) * HD ** (-0.5)
        scores = low_back(scores)
        query_pos = start + jnp.arange(block_rows, dtype=jnp.int32)
        key_pos = start - WINDOW + jnp.arange(WINDOW + block_rows, dtype=jnp.int32)
        allowed = (key_pos[None, :] <= query_pos[:, None]) & (query_pos[:, None] - key_pos[None, :] < WINDOW) & (key_pos[None, :] >= 0)
        scores = jnp.where(allowed, scores, -1e+30)
        weights = low(jax.nn.softmax(scores, axis=-1))
        mixed = jnp.einsum('chqk,ckd->qchd', weights, key_rows[:, :, HD:], precision=lax.Precision.HIGHEST)
        return mixed.reshape(block_rows, HEADS * HD)
    mixed = lax.map(jax.checkpoint(one_block), jnp.arange(N_FSDP, dtype=jnp.int32))
    mixed = low_back(low(mixed.reshape(seq_len, HEADS * HD)))
    return low_back(product(mixed, attend_output))

def feed_forward(normed, gate_weight, lift_weight, drop_weight):
    lowered = low(normed)
    gate_pre = low_back(product(lowered, gate_weight))
    lift_pre = low_back(product(lowered, lift_weight))
    hidden = low(smooth_gelu(gate_pre) * lift_pre)
    return low_back(product(hidden, drop_weight))

def recurrence(normed, recur_input, recur_branch, recur_output, temporal_kernel, decay_gate, input_gate, decay_rate):
    seq_len = normed.shape[0]
    lowered = low(normed)
    branch_x = low_back(low(product(lowered, recur_input)))
    branch_y = low_back(product(lowered, recur_branch))
    padded = jnp.concatenate([jnp.zeros((CONV - 1, RW), jnp.float32), branch_x], axis=0)
    conv_out = jnp.zeros((seq_len, RW), jnp.float32)
    for tap_index in range(CONV):
        conv_out = conv_out + temporal_kernel[tap_index] * padded[CONV - 1 - tap_index:CONV - 1 - tap_index + seq_len]
    blocked = low(conv_out).reshape(seq_len, RW // RB, RB)
    pre_decay = low_back(jnp.einsum('tnr,nrs->tns', blocked, decay_gate, precision=lax.Precision.HIGHEST).reshape(seq_len, RW))
    pre_admit = low_back(jnp.einsum('tnr,nrs->tns', blocked, input_gate, precision=lax.Precision.HIGHEST).reshape(seq_len, RW))
    factors, updates = gate_terms(pre_decay, pre_admit, conv_out, decay_rate)
    states = lax.associative_scan(compose, (factors, updates), axis=0)[1]
    states = low_back(low(states))
    merged = low(states * smooth_gelu(branch_y))
    return low_back(product(merged, recur_output))

def layers(sequence, valid, weights):
    attend_gain, query_weight, keyval_weight, attend_output, lower_gain, lower_gate, lower_lift, lower_drop, recur_gain, recur_input, recur_branch, recur_output, temporal_kernel, decay_gate, input_gate, decay_rate, upper_gain, upper_gate, upper_lift, upper_drop = weights
    first = sequence + attention(normalize(sequence, attend_gain), query_weight, keyval_weight, attend_output)
    second = first + feed_forward(normalize(first, lower_gain), lower_gate, lower_lift, lower_drop)
    third = second + recurrence(normalize(second, recur_gain), recur_input, recur_branch, recur_output, temporal_kernel, decay_gate, input_gate, decay_rate)
    fourth = third + feed_forward(normalize(third, upper_gain), upper_gate, upper_lift, upper_drop)
    return fourth * valid[:, None]

def reference(tokens, lengths, cotangent, attend_gain, query_weight, keyval_weight, attend_output, lower_gain, lower_gate, lower_lift, lower_drop, recur_gain, recur_input, recur_branch, recur_output, temporal_kernel, decay_gate, input_gate, decay_rate, upper_gain, upper_gate, upper_lift, upper_drop):
    weights = tuple((entry.astype(jnp.float32) for entry in (attend_gain, query_weight, keyval_weight, attend_output, lower_gain, lower_gate, lower_lift, lower_drop, recur_gain, recur_input, recur_branch, recur_output, temporal_kernel, decay_gate, input_gate, decay_rate, upper_gain, upper_gate, upper_lift, upper_drop)))

    def one_sequence(totals, inputs):
        sequence, cotangent_row, length = inputs
        valid = (jnp.arange(SLOTS, dtype=jnp.int32) < length).astype(jnp.float32)
        outputs, pullback = jax.vjp(lambda params, values: layers(values, valid, params), weights, sequence)
        weight_grads, input_grad = pullback(cotangent_row)
        totals = jax.tree.map(lambda left, right: left + right, totals, weight_grads)
        return (totals, (outputs, input_grad))
    zero_grads = jax.tree.map(jnp.zeros_like, weights)
    totals, stacked = lax.scan(one_sequence, zero_grads, (tokens.astype(jnp.float32), cotangent.astype(jnp.float32), lengths))
    outputs, input_grads = stacked
    return (outputs.astype(jnp.bfloat16), input_grads, totals[0], totals[1], totals[2], totals[3], totals[4], totals[5], totals[6], totals[7], totals[8], totals[9], totals[10], totals[11], totals[12], totals[13], totals[14], totals[15], totals[16], totals[17], totals[18], totals[19])
```

```python
import functools

import jax
import jax.numpy as jnp
from jax import lax
from jax.experimental import pallas as pl
from jax.experimental.pallas import tpu as pltpu
from jax.sharding import Mesh, PartitionSpec as P

WINDOW = 1024
EPSILON = 1e-06
DECAY_SCALE = 8.0

X = ("xh", "xl")
ZN = 4
F32 = jnp.float32
BF16 = jnp.bfloat16


def from_z(value, by):
    return lax.ppermute(value, "z", [((i + by) % ZN, i) for i in range(ZN)])


def to_z(value, by):
    return lax.ppermute(value, "z", [(i, (i + by) % ZN) for i in range(ZN)])


def swap(value):
    return lax.ppermute(value, "c", [(0, 1), (1, 0)])


def transpose_xz(value):
    pairs = [(x * ZN + z, z * ZN + x) for x in range(4) for z in range(ZN)]
    return lax.ppermute(value, ("xh", "xl", "z"), pairs)


def exchange_z(value):
    z = lax.axis_index("z")
    out = jnp.zeros_like(value)
    for r in range(ZN):
        piece = lax.dynamic_index_in_dim(value, (z + r) % ZN, 0, keepdims=True)
        if r:
            piece = to_z(piece, r)
        out = lax.dynamic_update_slice_in_dim(out, piece, (z + ZN - r) % ZN, 0)
    return out


def by_core(mine, other):
    first = lax.axis_index("c") == 0
    return jnp.where(first, mine, other), jnp.where(first, other, mine)


def core_pick(zero, one):
    return jnp.where(lax.axis_index("c") == 0, zero, one)


def core_join(mine, other):
    return jnp.concatenate(by_core(mine, other), axis=-1)


def normalize(values, gain):
    return values * lax.rsqrt(jnp.mean(values * values, axis=-1, keepdims=True) + EPSILON) * gain


def smooth_gelu(values):
    return jax.nn.gelu(values, approximate=True)


def gated_unit(gate_pre, lift_pre):
    return smooth_gelu(gate_pre) * lift_pre


def branch_merge(states, branch_y):
    return states * smooth_gelu(branch_y)


def gate_terms(pre_decay, pre_admit, conv_out, decay_rate):
    retain = jax.nn.sigmoid(pre_decay)
    admit = jax.nn.sigmoid(pre_admit)
    log_decay = -DECAY_SCALE * jax.nn.softplus(decay_rate) * (0.25 + retain)
    return (jnp.exp(log_decay), jnp.sqrt(-jnp.expm1(2.0 * log_decay)) * admit * conv_out)


def matmul(left, right):
    return jnp.dot(left, right, preferred_element_type=F32)


def times_transposed(left, right):
    return lax.dot_general(left, right, (((1,), (1,)), ((), ())), preferred_element_type=F32)


def transposed_times(left, right):
    return lax.dot_general(left, right, (((0,), (0,)), ((), ())), preferred_element_type=F32)


def gather_z(low):
    return [low] + [from_z(low, r) for r in range(1, ZN)]


def gather_rows(low):
    mine = gather_z(low)
    return jnp.concatenate(mine + [swap(block) for block in mine], axis=0)


def scatter_z(part):
    rows = part.shape[0] // ZN
    total = part[:rows].astype(F32)
    for r in range(1, ZN):
        total = total + to_z(part[r * rows : (r + 1) * rows].astype(BF16), r).astype(F32)
    return total


def scatter_rows(part):
    half = part.shape[0] // 2
    return scatter_z(part[:half] + swap(part[half:].astype(BF16)).astype(F32))


def kv_places(rows):
    places = []
    for x in range(4):
        for z in range(ZN):
            for j in range(2):
                position = ((x % 2) * ZN + 2 * (z // 2) + j) * 2 + x // 2
                places.append((x * ZN + z, j, z % 2, WINDOW + position * rows))
    return places


def attend_scores(pos_ref, q_ref, key_s, scale):
    rows, size = q_ref.shape[1], key_s.shape[1]
    heads = q_ref.shape[2] // size
    start = pl.multiple_of(pos_ref[pl.program_id(0)] * rows, rows)
    query = q_ref[0]
    query = jnp.concatenate([query[:, h * size : (h + 1) * size] for h in range(heads)], axis=0)
    key = key_s[pl.ds(start, WINDOW + rows), :]
    scores = times_transposed(query, key) * scale
    row = lax.broadcasted_iota(jnp.int32, scores.shape, 0) % rows
    col = lax.broadcasted_iota(jnp.int32, scores.shape, 1)
    allowed = (col > row) & (col <= row + WINDOW) & (col >= WINDOW - start)
    return start, query, key, jnp.where(allowed, scores, -1e30)


def load_kv(kv_ref, key_s, value_s):
    rows = kv_ref.shape[2]
    key_s[:WINDOW, :] = jnp.zeros((WINDOW, key_s.shape[1]), key_s.dtype)
    value_s[:WINDOW, :] = jnp.zeros((WINDOW, key_s.shape[1]), key_s.dtype)
    for source, j, kind, first in kv_places(rows):
        (value_s if kind else key_s)[first : first + rows, :] = kv_ref[source, j]


def attend_forward_kernel(scale, pos_ref, q_ref, kv_ref, out_ref, lse_ref, key_s, value_s):
    rows, size = q_ref.shape[1], key_s.shape[1]

    @pl.when(pl.program_id(0) == 0)
    def _():
        load_kv(kv_ref, key_s, value_s)

    start, query, key, scores = attend_scores(pos_ref, q_ref, key_s, scale)
    highest = jnp.max(scores, axis=-1, keepdims=True)
    lse = highest + jnp.log(jnp.sum(jnp.exp(scores - highest), axis=-1, keepdims=True))
    probs = jnp.exp(scores - lse).astype(BF16)
    mixed = matmul(probs, value_s[pl.ds(start, WINDOW + rows), :]).astype(BF16)
    out_ref[0] = jnp.concatenate(
        [mixed[h * rows : (h + 1) * rows] for h in range(q_ref.shape[2] // size)], axis=1
    )
    lse_ref[0] = lse


def attend_backward_kernel(
    scale, pos_ref, q_ref, kv_ref, grad_ref, lse_ref, dq_ref, dkv_ref, key_s, value_s, dk_s, dv_s
):
    rows, size = q_ref.shape[1], key_s.shape[1]
    heads = q_ref.shape[2] // size

    @pl.when(pl.program_id(0) == 0)
    def _():
        load_kv(kv_ref, key_s, value_s)
        dk_s[...] = jnp.zeros_like(dk_s)
        dv_s[...] = jnp.zeros_like(dv_s)

    start, query, key, scores = attend_scores(pos_ref, q_ref, key_s, scale)
    span = pl.ds(start, WINDOW + rows)
    probs = jnp.exp(scores - lse_ref[0])
    grad = grad_ref[0]
    grad = jnp.concatenate([grad[:, h * size : (h + 1) * size] for h in range(heads)], axis=0)
    prob_grad = times_transposed(grad, value_s[span, :])
    delta = jnp.sum(probs * prob_grad, axis=-1, keepdims=True)
    score_grad = (probs * (prob_grad - delta)).astype(BF16)
    query_grad = (matmul(score_grad, key) * scale).astype(BF16)
    dq_ref[0] = jnp.concatenate(
        [query_grad[h * rows : (h + 1) * rows] for h in range(heads)], axis=1
    )
    dk_s[span, :] += transposed_times(score_grad, query) * scale
    dv_s[span, :] += transposed_times(probs.astype(BF16), grad)

    @pl.when(pl.program_id(0) == pl.num_programs(0) - 1)
    def _():
        for source, j, kind, first in kv_places(rows):
            dkv_ref[source, j] = (dv_s if kind else dk_s)[first : first + rows, :].astype(BF16)


def whole(array):
    return pl.BlockSpec(array.shape, lambda r: (0,) * len(array.shape))


def by_block(*shape):
    return pl.BlockSpec((1,) + shape, lambda r: (r, 0, 0))


def kv_scratch(kv, dtype):
    return pltpu.VMEM((WINDOW + 16 * kv.shape[2], kv.shape[3]), dtype)


def attend_forward(positions, query, kv):
    blocks, rows, width = query.shape
    size = kv.shape[3]
    stacked = rows * (width // size)
    return pl.pallas_call(
        functools.partial(attend_forward_kernel, size**-0.5),
        grid=(blocks,),
        in_specs=[pl.BlockSpec(memory_space=pltpu.SMEM), by_block(rows, width), whole(kv)],
        out_specs=[by_block(rows, width), by_block(stacked, 1)],
        out_shape=[
            jax.ShapeDtypeStruct(query.shape, BF16),
            jax.ShapeDtypeStruct((blocks, stacked, 1), F32),
        ],
        scratch_shapes=[kv_scratch(kv, BF16), kv_scratch(kv, BF16)],
        compiler_params=pltpu.CompilerParams(vmem_limit_bytes=40 << 20),
    )(positions, query, kv)


def attend_backward(positions, query, kv, grad, lse):
    blocks, rows, width = query.shape
    size = kv.shape[3]
    stacked = rows * (width // size)
    return pl.pallas_call(
        functools.partial(attend_backward_kernel, size**-0.5),
        grid=(blocks,),
        in_specs=[
            pl.BlockSpec(memory_space=pltpu.SMEM),
            by_block(rows, width),
            whole(kv),
            by_block(rows, width),
            by_block(stacked, 1),
        ],
        out_specs=[by_block(rows, width), whole(kv)],
        out_shape=[
            jax.ShapeDtypeStruct(query.shape, BF16),
            jax.ShapeDtypeStruct(kv.shape, BF16),
        ],
        scratch_shapes=[
            kv_scratch(kv, BF16),
            kv_scratch(kv, BF16),
            kv_scratch(kv, F32),
            kv_scratch(kv, F32),
        ],
        compiler_params=pltpu.CompilerParams(vmem_limit_bytes=40 << 20),
    )(positions, query, kv, grad, lse)


def scan_kernel(backward, factor_ref, update_ref, state_ref):
    tiles = factor_ref.shape[0] // 8
    width = factor_ref.shape[1]
    row = lax.broadcasted_iota(jnp.int32, (8, width), 0)

    def turn(index, carry):
        tile = tiles - 1 - index if backward else index
        span = pl.ds(pl.multiple_of(tile * 8, 8), 8)
        factor, update = factor_ref[span, :], update_ref[span, :]
        for reach in (1, 2, 4):
            shift = 8 - reach if backward else reach
            inside = row < 8 - reach if backward else row >= reach
            far_update = pltpu.roll(update, shift, 0)
            far_factor = pltpu.roll(factor, shift, 0)
            update = jnp.where(inside, factor * far_update + update, update)
            factor = jnp.where(inside, factor * far_factor, factor)
        state = factor * carry + update
        state_ref[span, :] = state
        last = state[0:1] if backward else state[7:8]
        return jnp.broadcast_to(last, (8, width))

    lax.fori_loop(0, tiles, turn, jnp.zeros((8, width), F32), unroll=8)


def linear_scan(factors, updates, backward):
    return pl.pallas_call(
        functools.partial(scan_kernel, backward),
        out_shape=jax.ShapeDtypeStruct(factors.shape, F32),
        compiler_params=pltpu.CompilerParams(vmem_limit_bytes=24 << 20),
    )(factors, updates)


def to_sequence(part, blocks):
    rows = part.shape[0] // 8
    width = part.shape[1] // blocks
    z = lax.axis_index("z")
    sent = part.reshape(2, ZN, rows, blocks, width).transpose(0, 3, 1, 2, 4)
    got = lax.all_to_all(sent.reshape(4, ZN, rows, width), X, 0, 0)
    got = jnp.roll(got, z, axis=1).reshape(2, 2, ZN, rows, width)
    return got.transpose(1, 2, 0, 3, 4).reshape(16 * rows, width)


def from_sequence(values, blocks):
    rows, width = values.shape[0] // 16, values.shape[1]
    z = lax.axis_index("z")
    sent = values.reshape(2, ZN, 2, rows, width).transpose(2, 0, 1, 3, 4)
    sent = jnp.roll(sent.reshape(4, ZN, rows, width), -z, axis=1)
    got = lax.all_to_all(sent, X, 0, 0).reshape(2, blocks, ZN, rows, width)
    return got.transpose(0, 2, 3, 1, 4).reshape(8 * rows, blocks * width)


def shift_down(values, by):
    if by == 0:
        return values
    return jnp.concatenate([jnp.zeros_like(values[:by]), values[:-by]], axis=0)


def shift_up(values, by):
    if by == 0:
        return values
    return jnp.concatenate([values[by:], jnp.zeros_like(values[:by])], axis=0)


def unit_slices(weight):
    quarter = weight.shape[1] // ZN
    wide = quarter * 5 // 9
    skip = quarter - wide
    keep = lax.broadcasted_iota(jnp.int32, (weight.shape[0], wide), 1) >= wide - skip
    picked = []
    for member in range(ZN):
        columns = weight[:, member * quarter : (member + 1) * quarter]
        picked.append(core_pick(columns[:, :wide], jnp.where(keep, columns[:, skip:], 0)))
    return jnp.stack(picked)


def half_slices(weight):
    quarter = weight.shape[1] // ZN
    half = quarter // 2
    picked = []
    for member in range(ZN):
        columns = weight[:, member * quarter : (member + 1) * quarter]
        picked.append(core_pick(columns[:, :half], columns[:, half:]))
    return jnp.stack(picked)


def own_half(weight):
    half = weight.shape[-1] // 2
    return core_pick(weight[..., :half], weight[..., half:])


def other_half(weight):
    half = weight.shape[-1] // 2
    return core_pick(weight[..., half:], weight[..., :half])


def gather_x(value):
    return lax.all_gather(value, X, axis=0, tiled=True)


def columns_of(picked):
    turned = exchange_z(picked)
    return gather_x(turned.reshape(-1, turned.shape[2]))


def core_rows(stacked, wide):
    skip = stacked.shape[0] - wide
    low, high = stacked[:wide], stacked[skip:]
    return core_join(core_pick(low, high), swap(core_pick(high, low)))


def reduce_columns(grad):
    part = lax.psum_scatter(grad.astype(BF16), X, scatter_dimension=0, tiled=True)
    part = lax.psum(part, "y")
    return exchange_z(part.reshape(ZN, part.shape[0] // ZN, part.shape[1]))


def reduce_rows(grad):
    part = lax.psum_scatter(grad.astype(BF16), X, scatter_dimension=0, tiled=True)
    part = transpose_xz(lax.psum(part, "y"))
    return core_join(part, swap(part)).astype(F32)


def unit_grads(grad):
    mine = reduce_columns(grad)
    zero, one = by_core(mine, swap(mine))
    wide = grad.shape[1] // 2
    skip = wide * 4 // 5
    gates, lifts = [], []
    for member in range(ZN):
        for out, first in ((gates, 0), (lifts, wide)):
            out.append(zero[member, :, first : first + wide])
            out.append(one[member, :, first + wide - skip : first + wide])
    return (
        jnp.concatenate(gates, axis=1).astype(F32),
        jnp.concatenate(lifts, axis=1).astype(F32),
    )


def half_grads(grad):
    mine = reduce_columns(grad)
    zero, one = by_core(mine, swap(mine))
    half = grad.shape[1] // 2
    outs = []
    for first in (0, half):
        pieces = []
        for member in range(ZN):
            pieces.append(zero[member, :, first : first + half])
            pieces.append(one[member, :, first : first + half])
        outs.append(jnp.concatenate(pieces, axis=1).astype(F32))
    return outs


def member_rows(grad, wide):
    low = grad.astype(BF16)
    zero, one = by_core(own_half(low), swap(other_half(low)))
    return jnp.concatenate([zero, one[zero.shape[0] - wide :]], axis=0)


def dense_forward(residual, gain, unit_weight, drop_weight):
    normed, norm_pull = jax.vjp(normalize, residual, gain)
    rows = gather_rows(normed.astype(BF16))
    pre = matmul(rows, unit_weight)
    wide = pre.shape[1] // 2
    hidden, unit_pull = jax.vjp(gated_unit, pre[:, :wide], pre[:, wide:])
    hidden_low = hidden.astype(BF16)
    out = residual + scatter_rows(matmul(hidden_low, drop_weight))
    return out, (norm_pull, rows, unit_pull, hidden_low)


def dense_backward(residual_grad, stored, unit_weight, drop_weight):
    norm_pull, rows, unit_pull, hidden_low = stored
    grad_rows = gather_rows(residual_grad.astype(BF16))
    hidden_grad = times_transposed(grad_rows, drop_weight)
    pre_low = jnp.concatenate([part.astype(BF16) for part in unit_pull(hidden_grad)], axis=1)
    normed_grad = scatter_rows(times_transposed(pre_low, unit_weight))
    input_grad, gain_grad = norm_pull(normed_grad)
    unit_grad = transposed_times(rows, pre_low)
    drop_grad = transposed_times(hidden_low, grad_rows)
    wide = drop_grad.shape[0]
    gate_grad, lift_grad = unit_grads(unit_grad)
    drop_grad = reduce_rows(member_rows(drop_grad, wide * 4 // 5))
    return residual_grad + input_grad, gain_grad, (gate_grad, lift_grad, drop_grad)


def body(
    tokens,
    lengths,
    cotangent,
    attend_gain,
    query_weight,
    keyval_weight,
    attend_output,
    lower_gain,
    lower_gate,
    lower_lift,
    lower_drop,
    recur_gain,
    recur_input,
    recur_branch,
    recur_output,
    temporal_kernel,
    decay_gate,
    input_gate,
    decay_rate,
    upper_gain,
    upper_gate,
    upper_lift,
    upper_drop,
):
    c, xh, xl, z = (lax.axis_index(name) for name in ("c", "xh", "xl", "z"))
    row_count, features = tokens.shape[1:]
    size = keyval_weight.shape[1] // 2
    query_width = query_weight.shape[1] // ZN
    drop_rows, recur_rows = lower_drop.shape[0], recur_output.shape[0]
    channels = 2 * recur_rows
    tap_count = temporal_kernel.shape[0]
    even = z % 2 == 0
    positions = ((xl * ZN + (z + jnp.arange(ZN, dtype=jnp.int32)) % ZN) * 2 + xh).astype(jnp.int32)
    token_pos = positions[0] * row_count + jnp.arange(row_count, dtype=jnp.int32)
    valid = (token_pos < lengths[0]).astype(F32)[:, None]

    member_query = query_weight.reshape(-1, ZN, query_width).transpose(1, 0, 2)
    member_kv = jnp.stack([keyval_weight[:, (m % 2) * size : (m % 2 + 1) * size] for m in range(ZN)])
    attend_columns = jnp.concatenate([member_query, member_kv], axis=2)
    half_in = columns_of(own_half(attend_columns))
    half_out = gather_x(transpose_xz(own_half(attend_output)))
    attend_in = core_join(half_in, swap(half_in))
    attend_out = core_join(half_out, swap(half_out))

    lower_unit = columns_of(
        jnp.concatenate([unit_slices(lower_gate), unit_slices(lower_lift)], axis=2)
    )
    upper_columns = columns_of(
        jnp.concatenate(
            [
                unit_slices(upper_gate),
                unit_slices(upper_lift),
                half_slices(recur_input),
                half_slices(recur_branch),
            ],
            axis=2,
        )
    )
    unit_width = lower_unit.shape[1]
    wide = unit_width // 2
    upper_unit = upper_columns[:, :unit_width]
    recur_in = upper_columns[:, unit_width:]
    drops = transpose_xz(
        own_half(jnp.concatenate([lower_drop, recur_output, upper_drop], axis=0))
    )
    drops = lax.all_gather(drops, X, axis=0, tiled=False)
    half_width = features // 2
    lower_down = core_rows(drops[:, :drop_rows].reshape(-1, half_width), wide)
    recur_out = core_rows(
        drops[:, drop_rows : drop_rows + recur_rows].reshape(-1, half_width), channels
    )
    upper_down = core_rows(drops[:, drop_rows + recur_rows :].reshape(-1, half_width), wide)

    start_rows = tokens[0].astype(F32)
    normed_attend, attend_pull = jax.vjp(normalize, start_rows, attend_gain)
    attend_rows = jnp.concatenate(gather_z(normed_attend.astype(BF16)), axis=0)
    mixed_in = matmul(attend_rows, attend_in).astype(BF16).reshape(ZN, row_count, -1)
    queries = mixed_in[:, :, :query_width]
    kv_part = mixed_in[:, :, query_width:]
    kv_send = jnp.stack(
        [jnp.where(even, kv_part[0], kv_part[3]), jnp.where(even, kv_part[1], kv_part[0])]
    )
    kv = lax.all_to_all(
        jnp.broadcast_to(kv_send[None], (16,) + kv_send.shape), X + ("z",), 0, 0
    )
    attended, log_total = attend_forward(positions, queries, kv)
    attend_back = attended.reshape(ZN * row_count, query_width)
    first_rows = start_rows + scatter_z(matmul(attend_back, attend_out))

    second_rows, lower_kept = dense_forward(first_rows, lower_gain, lower_unit, lower_down)

    normed_recur, recur_pull = jax.vjp(normalize, second_rows, recur_gain)
    recur_low_rows = gather_rows(normed_recur.astype(BF16))
    branches = matmul(recur_low_rows, recur_in)
    branch_y = branches[:, channels:]
    x_seq = to_sequence(branches[:, :channels].astype(BF16), 2).astype(F32)
    block = (z * 2 + c) * 2 + xl
    width = decay_gate.shape[1]
    own_decay = lax.dynamic_slice_in_dim(decay_rate, block * width, width, 0)
    own_taps = lax.dynamic_slice_in_dim(temporal_kernel, block * width, width, 1)
    own_decay_gate = lax.dynamic_index_in_dim(decay_gate, block, 0, keepdims=False)
    own_input_gate = lax.dynamic_index_in_dim(input_gate, block, 0, keepdims=False)
    shifted = [shift_down(x_seq, k) for k in range(tap_count)]
    conv_out = sum(own_taps[k] * shifted[k] for k in range(tap_count))
    conv_low = conv_out.astype(BF16)
    pre_decay = matmul(conv_low, own_decay_gate)
    pre_admit = matmul(conv_low, own_input_gate)
    (factors, updates), gate_pull = jax.vjp(gate_terms, pre_decay, pre_admit, conv_out, own_decay)
    states = linear_scan(factors, updates, False)
    states_back = from_sequence(states.astype(BF16), 2)
    merged, merge_pull = jax.vjp(branch_merge, states_back.astype(F32), branch_y)
    merged_low = merged.astype(BF16)
    third_rows = second_rows + scatter_rows(matmul(merged_low, recur_out))

    fourth_rows, upper_kept = dense_forward(third_rows, upper_gain, upper_unit, upper_down)
    out_tokens = (fourth_rows * valid).astype(BF16)[None]

    residual_grad = cotangent[0].astype(F32) * valid
    residual_grad, grad_upper_gain, upper_grads = dense_backward(
        residual_grad, upper_kept, upper_unit, upper_down
    )

    recur_grad_rows = gather_rows(residual_grad.astype(BF16))
    merged_grad = times_transposed(recur_grad_rows, recur_out)
    states_grad, branch_y_grad = merge_pull(merged_grad)
    state_grad = to_sequence(states_grad.astype(BF16), 2).astype(F32)
    adjoint = linear_scan(shift_up(factors, 1), state_grad, True)
    decay_grad, admit_grad, conv_grad, own_decay_grad = gate_pull(
        (adjoint * shift_down(states, 1), adjoint)
    )
    decay_grad_low, admit_grad_low = decay_grad.astype(BF16), admit_grad.astype(BF16)
    conv_grad = (
        conv_grad
        + times_transposed(decay_grad_low, own_decay_gate)
        + times_transposed(admit_grad_low, own_input_gate)
    )
    own_gate_grad = transposed_times(conv_low, decay_grad_low)
    own_admit_grad = transposed_times(conv_low, admit_grad_low)
    tap_grads = jnp.stack([jnp.sum(conv_grad * shifted[k], axis=0) for k in range(tap_count)])
    x_seq_grad = sum(own_taps[k] * shift_up(conv_grad, k) for k in range(tap_count))
    branch_x_grad = from_sequence(x_seq_grad.astype(BF16), 2)
    branch_grad = jnp.concatenate([branch_x_grad, branch_y_grad.astype(BF16)], axis=1)
    normed_grad = scatter_rows(times_transposed(branch_grad, recur_in))
    recur_input_grad, grad_recur_gain = recur_pull(normed_grad)
    grad_recur_input, grad_recur_branch = half_grads(transposed_times(recur_low_rows, branch_grad))
    grad_recur_output = reduce_rows(
        member_rows(transposed_times(merged_low, recur_grad_rows), channels)
    )
    residual_grad = residual_grad + recur_input_grad
    channel_grads = jnp.concatenate(
        [
            own_gate_grad,
            own_admit_grad,
            tap_grads,
            own_decay_grad[None],
            jnp.zeros((3, width), F32),
        ],
        axis=0,
    )
    channel_grads = lax.all_gather(lax.psum(channel_grads, ("y", "xh")), ("z", "c", "xl"), axis=0)
    grad_decay_gate = channel_grads[:, :width]
    grad_input_gate = channel_grads[:, width : 2 * width]
    grad_temporal_kernel = (
        channel_grads[:, 2 * width : 2 * width + tap_count]
        .transpose(1, 0, 2)
        .reshape(tap_count, -1)
    )
    grad_decay_rate = channel_grads[:, 2 * width + tap_count].reshape(-1)

    residual_grad, grad_lower_gain, lower_grads = dense_backward(
        residual_grad, lower_kept, lower_unit, lower_down
    )

    grad_rows = jnp.concatenate(gather_z(residual_grad.astype(BF16)), axis=0)
    attend_grad = times_transposed(grad_rows, attend_out).astype(BF16)
    query_grad, kv_grad = attend_backward(
        positions, queries, kv, attend_grad.reshape(queries.shape), log_total
    )
    kv_grad = lax.all_to_all(kv_grad, X + ("z",), 0, 0)
    kv_grad = jnp.sum(kv_grad.astype(F32), axis=0).astype(BF16)
    nothing = jnp.zeros_like(kv_grad[0])
    kv_grad = jnp.stack(
        [
            jnp.where(even, kv_grad[0], kv_grad[1]),
            jnp.where(even, kv_grad[1], nothing),
            nothing,
            jnp.where(even, nothing, kv_grad[0]),
        ]
    )
    mixed_grad = jnp.concatenate([query_grad, kv_grad], axis=2).reshape(ZN * row_count, -1)
    normed_grad = scatter_z(times_transposed(mixed_grad, attend_in))
    in_grad = transposed_times(attend_rows, mixed_grad).astype(BF16)
    out_grad = transposed_times(attend_back, grad_rows).astype(BF16)
    in_grad = own_half(in_grad).astype(F32) + swap(other_half(in_grad)).astype(F32)
    out_grad = own_half(out_grad).astype(F32) + swap(other_half(out_grad)).astype(F32)
    grad_attend_output = reduce_rows(out_grad)
    in_grad = reduce_columns(in_grad)
    in_grad = core_join(in_grad, swap(in_grad)).astype(F32)
    grad_query_weight = jnp.concatenate([in_grad[m, :, :query_width] for m in range(ZN)], axis=1)
    grad_keyval_weight = jnp.concatenate(
        [in_grad[m, :, query_width:] + in_grad[m + 2, :, query_width:] for m in range(2)], axis=1
    )
    attend_input_grad, grad_attend_gain = attend_pull(normed_grad)
    residual_grad = residual_grad + attend_input_grad
    gains = lax.psum(
        jnp.stack([grad_attend_gain, grad_lower_gain, grad_recur_gain, grad_upper_gain]),
        ("y", "c", "xh", "xl", "z"),
    )
    return (
        out_tokens,
        residual_grad[None],
        gains[0],
        grad_query_weight,
        grad_keyval_weight,
        grad_attend_output,
        gains[1],
        *lower_grads,
        gains[2],
        grad_recur_input,
        grad_recur_branch,
        grad_recur_output,
        grad_temporal_kernel,
        grad_decay_gate,
        grad_input_gate,
        grad_decay_rate,
        gains[3],
        *upper_grads,
    )


def solution(mesh):
    grid = Mesh(mesh.devices.reshape(-1, 2, 2, 2, ZN), ("y", "c", "xh", "xl", "z"))
    rows = P(("y", "c"), ("xl", "z", "xh"), None)
    weight = P(("xh", "xl", "z"), None)
    same = P()
    return jax.shard_map(
        body,
        mesh=grid,
        in_specs=(
            (rows, P(("y", "c")), rows)
            + (same, weight, weight, weight)
            + (same, weight, weight, weight)
            + (same, weight, weight, weight, same, same, same, same)
            + (same, weight, weight, weight)
        ),
        out_specs=(
            (rows, rows)
            + (same, weight, weight, weight)
            + (same, weight, weight, weight)
            + (same, weight, weight, weight, same, same, same, same)
            + (same, weight, weight, weight)
        ),
        check_vma=False,
    )
```

```python
import functools
import math

import jax
import jax.numpy as jnp
from jax import lax
from jax.experimental import pallas as pl
from jax.experimental.pallas import tpu as pltpu
from jax.sharding import Mesh, PartitionSpec as P

WINDOW = 1024
EPSILON = 1e-06
DECAY_SCALE = 8.0

X = ("xh", "xl")
XN = 4
F32 = jnp.float32
BF16 = jnp.bfloat16


def x_index():
    return lax.axis_index("xh") * 2 + lax.axis_index("xl")


def from_x(value, by):
    return lax.ppermute(value, X, [((i + by) % XN, i) for i in range(XN)])


def to_x(value, by):
    return lax.ppermute(value, X, [(i, (i + by) % XN) for i in range(XN)])


def flip(value, axis, by):
    return lax.ppermute(value, axis, [(i, i ^ by) for i in range(lax.axis_size(axis))])


def tie(main, *side):
    return lax.optimization_barrier((main, *side))


def after(value, *done):
    return lax.optimization_barrier((value, done))[0]


def swap(value):
    return lax.ppermute(value, "c", [(0, 1), (1, 0)])


def exchange_x(value):
    return lax.all_to_all(value, X, 0, 0)


def by_core(mine, other):
    first = lax.axis_index("c") == 0
    return jnp.where(first, mine, other), jnp.where(first, other, mine)


def core_pick(zero, one):
    return jnp.where(lax.axis_index("c") == 0, zero, one)


def core_join(mine, other):
    return jnp.concatenate(by_core(mine, other), axis=-1)


def normalize(values, gain):
    return values * lax.rsqrt(jnp.mean(values * values, axis=-1, keepdims=True) + EPSILON) * gain


def smooth_gelu(values):
    return jax.nn.gelu(values, approximate=True)


def gated_unit(gate_pre, lift_pre):
    return smooth_gelu(gate_pre) * lift_pre


def branch_merge(states, branch_y):
    return states * smooth_gelu(branch_y)


def gate_terms(pre_decay, pre_admit, conv_out, decay_rate):
    retain = jax.nn.sigmoid(pre_decay)
    admit = jax.nn.sigmoid(pre_admit)
    log_decay = -DECAY_SCALE * jax.nn.softplus(decay_rate) * (0.25 + retain)
    return (jnp.exp(log_decay), jnp.sqrt(-jnp.expm1(2.0 * log_decay)) * admit * conv_out)


def matmul(left, right):
    return jnp.dot(left, right, preferred_element_type=F32)


def times_transposed(left, right):
    return lax.dot_general(left, right, (((1,), (1,)), ((), ())), preferred_element_type=F32)


def transposed_times(left, right):
    return lax.dot_general(left, right, (((0,), (0,)), ((), ())), preferred_element_type=F32)


def gather_rows(low):
    return [low] + [from_x(low, r) for r in range(1, XN)]


def chunked(low, begin, end, side=()):
    near = {1: from_x(low, 1), 3: from_x(low, 3)}
    first, later = tie(begin(0, low), low)
    far, side = tie(from_x(later, 2), side)
    chunks = [low, near[1], far, near[3]]
    outs = [end(0, first)] + [None] * (XN - 1)
    for k in (1, 3, 2):
        outs[k] = end(k, begin(k, chunks[k]))
    return chunks, outs, side


def scatter_chunks(parts):
    total = parts[0]
    for r in (2, 1, 3):
        total = total + to_x(parts[r].astype(BF16), r).astype(F32)
    return total


def cost(microseconds):
    return pl.CostEstimate(flops=0, bytes_accessed=int(microseconds * 3.6e6), transcendentals=0)


def core_scalar():
    return lax.axis_index("c").astype(jnp.int32)[None]


def product_kernel(count, pieces, split, core_ref, *refs):
    lefts, rights = refs[:count], refs[count : 2 * count]
    mine_ref, other_ref, right = refs[2 * count :]
    rows = lefts[0].shape[0]

    @pl.when(pl.program_id(0) == 0)
    def _():
        for k in range(count):
            right[k * rows : (k + 1) * rows, :] = rights[k][...]

    left = jnp.concatenate([ref[...] for ref in lefts], axis=0)
    total = transposed_times(left, right[...]).astype(BF16)
    first = core_ref[0] == 0
    at = 0
    for low, high, width in pieces:
        zero, one = total[:, low : low + width], total[:, high : high + width]
        for ref, value in ((mine_ref, jnp.where(first, zero, one)), (other_ref, jnp.where(first, one, zero))):
            if split:
                each = ref.shape[2]
                for z in range(ref.shape[0]):
                    ref[z, 0, :, at : at + width] = value[z * each : (z + 1) * each]
            else:
                ref[:, at : at + width] = value
        at += width


def chunk_product(lefts, rights, pieces, split):
    rows, deep = lefts[0].shape
    width = rights[0].shape[1]
    count = len(lefts)
    kept = sum(piece[2] for piece in pieces)
    if split:
        tile = deep // XN
        shape = (4, XN, tile // 4, kept)
        spec = pl.BlockSpec((4, 1, tile // 4, kept), lambda i: (0, i, 0, 0))
    else:
        tile = next((t for t in (384, 256, 128) if deep % t == 0), deep)
        shape = (deep, kept)
        spec = pl.BlockSpec((tile, kept), lambda i: (i, 0))
    mine, other = pl.pallas_call(
        functools.partial(product_kernel, count, pieces, split),
        grid=(deep // tile,),
        in_specs=[pl.BlockSpec(memory_space=pltpu.SMEM)]
        + [pl.BlockSpec((rows, tile), lambda i: (0, i)) for _ in lefts]
        + [pl.BlockSpec((rows, width), lambda i: (0, 0)) for _ in rights],
        out_specs=[spec, spec],
        out_shape=[jax.ShapeDtypeStruct(shape, BF16)] * 2,
        scratch_shapes=[pltpu.VMEM((count * rows, width), BF16)],
        compiler_params=pltpu.CompilerParams(vmem_limit_bytes=48 << 20),
        cost_estimate=pl.CostEstimate(
            flops=2 * count * rows * deep * width,
            bytes_accessed=2 * (count * rows * (deep + width) + 2 * deep * kept),
            transcendentals=0,
        ),
    )(core_scalar(), *lefts, *rights)
    total = (mine.astype(F32) + swap(other).astype(F32)).astype(BF16)
    return total.reshape(-1, kept)


def unit_pieces(quarter):
    wide = quarter * 5 // 9
    return ((0, quarter - wide, wide), (quarter, 2 * quarter - wide, wide))


def half_pieces(width):
    half = width // 4
    return ((0, half, half), (2 * half, 3 * half, half))


def row_pieces(width):
    return ((0, width // 2, width // 2),)


def kv_places(rows):
    places = []
    for x in range(XN):
        for z in range(4):
            for j in range(2):
                position = (j * 4 + z) * 2 + x // 2
                places.append((x * 4 + z, j, x % 2, WINDOW + position * rows))
    return places


def attend_scores(pos_ref, q_ref, key_s, scale):
    rows, size = q_ref.shape[1], key_s.shape[1]
    heads = q_ref.shape[2] // size
    start = pl.multiple_of(pos_ref[pl.program_id(0)] * rows, rows)
    query = q_ref[0]
    query = jnp.concatenate([query[:, h * size : (h + 1) * size] for h in range(heads)], axis=0)
    key = key_s[pl.ds(start, WINDOW + rows), :]
    scores = times_transposed(query, key) * scale
    row = lax.broadcasted_iota(jnp.int32, scores.shape, 0) % rows
    col = lax.broadcasted_iota(jnp.int32, scores.shape, 1)
    allowed = (col > row) & (col <= row + WINDOW) & (col >= WINDOW - start)
    return start, query, key, jnp.where(allowed, scores, -1e30)


def load_kv(kv_ref, key_s, value_s):
    rows = kv_ref.shape[2]
    key_s[:WINDOW, :] = jnp.zeros((WINDOW, key_s.shape[1]), key_s.dtype)
    value_s[:WINDOW, :] = jnp.zeros((WINDOW, key_s.shape[1]), key_s.dtype)
    for source, j, kind, first in kv_places(rows):
        (value_s if kind else key_s)[first : first + rows, :] = kv_ref[source, j]


def attend_forward_kernel(scale, pos_ref, q_ref, kv_ref, out_ref, lse_ref, key_s, value_s):
    rows, size = q_ref.shape[1], key_s.shape[1]

    @pl.when(pl.program_id(0) == 0)
    def _():
        load_kv(kv_ref, key_s, value_s)

    start, query, key, scores = attend_scores(pos_ref, q_ref, key_s, scale)
    highest = jnp.max(scores, axis=-1, keepdims=True)
    lse = highest + jnp.log(jnp.sum(jnp.exp(scores - highest), axis=-1, keepdims=True))
    probs = jnp.exp(scores - lse).astype(BF16)
    mixed = matmul(probs, value_s[pl.ds(start, WINDOW + rows), :]).astype(BF16)
    out_ref[0] = jnp.concatenate(
        [mixed[h * rows : (h + 1) * rows] for h in range(q_ref.shape[2] // size)], axis=1
    )
    lse_ref[0] = lse


def attend_backward_kernel(
    scale, pos_ref, q_ref, kv_ref, grad_ref, lse_ref, dq_ref, dkv_ref, key_s, value_s, dk_s, dv_s
):
    rows, size = q_ref.shape[1], key_s.shape[1]
    heads = q_ref.shape[2] // size

    @pl.when(pl.program_id(0) == 0)
    def _():
        load_kv(kv_ref, key_s, value_s)
        dk_s[...] = jnp.zeros_like(dk_s)
        dv_s[...] = jnp.zeros_like(dv_s)

    start, query, key, scores = attend_scores(pos_ref, q_ref, key_s, scale)
    span = pl.ds(start, WINDOW + rows)
    probs = jnp.exp(scores - lse_ref[0])
    grad = grad_ref[0]
    grad = jnp.concatenate([grad[:, h * size : (h + 1) * size] for h in range(heads)], axis=0)
    prob_grad = times_transposed(grad, value_s[span, :])
    delta = jnp.sum(probs * prob_grad, axis=-1, keepdims=True)
    score_grad = (probs * (prob_grad - delta)).astype(BF16)
    query_grad = (matmul(score_grad, key) * scale).astype(BF16)
    dq_ref[0] = jnp.concatenate(
        [query_grad[h * rows : (h + 1) * rows] for h in range(heads)], axis=1
    )
    dk_s[span, :] += transposed_times(score_grad, query) * scale
    dv_s[span, :] += transposed_times(probs.astype(BF16), grad)

    @pl.when(pl.program_id(0) == pl.num_programs(0) - 1)
    def _():
        for source, j, kind, first in kv_places(rows):
            dkv_ref[source, j] = (dv_s if kind else dk_s)[first : first + rows, :].astype(BF16)


def whole(array):
    return pl.BlockSpec(array.shape, lambda r: (0,) * len(array.shape))


def by_block(*shape):
    return pl.BlockSpec((1,) + shape, lambda r: (r, 0, 0))


def kv_scratch(kv, dtype):
    return pltpu.VMEM((WINDOW + 16 * kv.shape[2], kv.shape[3]), dtype)


def attend_forward(positions, query, kv):
    blocks, rows, width = query.shape
    size = kv.shape[3]
    stacked = rows * (width // size)
    return pl.pallas_call(
        functools.partial(attend_forward_kernel, size**-0.5),
        grid=(blocks,),
        in_specs=[pl.BlockSpec(memory_space=pltpu.SMEM), by_block(rows, width), whole(kv)],
        out_specs=[by_block(rows, width), by_block(stacked, 1)],
        out_shape=[
            jax.ShapeDtypeStruct(query.shape, BF16),
            jax.ShapeDtypeStruct((blocks, stacked, 1), F32),
        ],
        scratch_shapes=[kv_scratch(kv, BF16), kv_scratch(kv, BF16)],
        cost_estimate=cost(7),
        compiler_params=pltpu.CompilerParams(vmem_limit_bytes=40 << 20),
    )(positions, query, kv)


def attend_backward(positions, query, kv, grad, lse):
    blocks, rows, width = query.shape
    size = kv.shape[3]
    stacked = rows * (width // size)
    return pl.pallas_call(
        functools.partial(attend_backward_kernel, size**-0.5),
        grid=(blocks,),
        in_specs=[
            pl.BlockSpec(memory_space=pltpu.SMEM),
            by_block(rows, width),
            whole(kv),
            by_block(rows, width),
            by_block(stacked, 1),
        ],
        out_specs=[by_block(rows, width), whole(kv)],
        out_shape=[
            jax.ShapeDtypeStruct(query.shape, BF16),
            jax.ShapeDtypeStruct(kv.shape, BF16),
        ],
        scratch_shapes=[
            kv_scratch(kv, BF16),
            kv_scratch(kv, BF16),
            kv_scratch(kv, F32),
            kv_scratch(kv, F32),
        ],
        cost_estimate=cost(9),
        compiler_params=pltpu.CompilerParams(vmem_limit_bytes=40 << 20),
    )(positions, query, kv, grad, lse)


def scan_kernel(backward, factor_ref, update_ref, state_ref):
    tiles = factor_ref.shape[0] // 8
    width = factor_ref.shape[1]
    row = lax.broadcasted_iota(jnp.int32, (8, width), 0)

    def turn(index, carry):
        tile = tiles - 1 - index if backward else index
        span = pl.ds(pl.multiple_of(tile * 8, 8), 8)
        factor, update = factor_ref[span, :], update_ref[span, :]
        for reach in (1, 2, 4):
            shift = 8 - reach if backward else reach
            inside = row < 8 - reach if backward else row >= reach
            far_update = pltpu.roll(update, shift, 0)
            far_factor = pltpu.roll(factor, shift, 0)
            update = jnp.where(inside, factor * far_update + update, update)
            factor = jnp.where(inside, factor * far_factor, factor)
        state = factor * carry + update
        state_ref[span, :] = state
        last = state[0:1] if backward else state[7:8]
        return jnp.broadcast_to(last, (8, width))

    lax.fori_loop(0, tiles, turn, jnp.zeros((8, width), F32), unroll=8)


def linear_scan(factors, updates, backward):
    return pl.pallas_call(
        functools.partial(scan_kernel, backward),
        out_shape=jax.ShapeDtypeStruct(factors.shape, F32),
        cost_estimate=cost(1.5),
        compiler_params=pltpu.CompilerParams(vmem_limit_bytes=24 << 20),
    )(factors, updates)


def to_sequence(chunks):
    rows, width = chunks[0].shape[0], chunks[0].shape[1] // 4
    sent = jnp.stack(
        [jnp.stack([part[:, b * width : (b + 1) * width] for part in chunks]) for b in range(4)]
    )
    got = lax.all_to_all(sent, "z", 0, 0)
    got = jnp.roll(got, x_index(), axis=1).reshape(4, 2, 2, rows, width)
    return got.transpose(2, 0, 1, 3, 4).reshape(16 * rows, width)


def from_sequence(values):
    rows, width = values.shape[0] // 16, values.shape[1]
    sent = values.reshape(2, 4, 2, rows, width).transpose(1, 2, 0, 3, 4)
    sent = jnp.roll(sent.reshape(4, XN, rows, width), -x_index(), axis=1)
    got = lax.all_to_all(sent, "z", 0, 0)
    return [jnp.concatenate([got[b, k] for b in range(4)], axis=1) for k in range(XN)]


def shift_down(values, by):
    if by == 0:
        return values
    return jnp.concatenate([jnp.zeros_like(values[:by]), values[:-by]], axis=0)


def shift_up(values, by):
    if by == 0:
        return values
    return jnp.concatenate([values[by:], jnp.zeros_like(values[:by])], axis=0)


def unit_slices(weight):
    quarter = weight.shape[1] // XN
    wide = quarter * 5 // 9
    skip = quarter - wide
    keep = lax.broadcasted_iota(jnp.int32, (weight.shape[0], wide), 1) >= wide - skip
    picked = []
    for member in range(XN):
        columns = weight[:, member * quarter : (member + 1) * quarter]
        picked.append(core_pick(columns[:, :wide], jnp.where(keep, columns[:, skip:], 0)))
    return jnp.stack(picked)


def half_slices(weight):
    quarter = weight.shape[1] // XN
    half = quarter // 2
    picked = []
    for member in range(XN):
        columns = weight[:, member * quarter : (member + 1) * quarter]
        picked.append(core_pick(columns[:, :half], columns[:, half:]))
    return jnp.stack(picked)


def own_half(weight):
    half = weight.shape[-1] // 2
    return core_pick(weight[..., :half], weight[..., half:])


def other_half(weight):
    half = weight.shape[-1] // 2
    return core_pick(weight[..., half:], weight[..., :half])


def gather_direct(value):
    z = lax.axis_index("z")
    out = jnp.zeros((value.shape[0], 4) + value.shape[1:], value.dtype)
    for by in range(4):
        piece = flip(value, "z", by) if by else value
        out = lax.dynamic_update_slice_in_dim(out, piece[:, None], z ^ by, 1)
    return out


def row_join(rows):
    return core_join(rows, swap(rows))


def join_kernel(plans, core_ref, mine_ref, other_ref, *outs):
    first = core_ref[0] == 0
    each = mine_ref.shape[2]
    for z in range(mine_ref.shape[0]):
        mine, other = mine_ref[z, 0], other_ref[z, 0]
        zero, one = jnp.where(first, mine, other), jnp.where(first, other, mine)
        for out, pieces in zip(outs, plans):
            at = 0
            for core, low, high in pieces:
                out[z * each : (z + 1) * each, at : at + high - low] = (one if core else zero)[:, low:high]
                at += high - low


def column_join(columns, plans):
    zs, xs, rows, width = columns.shape
    spec = pl.BlockSpec((zs, 1, rows, width), lambda i: (0, i, 0, 0))
    widths = [sum(high - low for _, low, high in pieces) for pieces in plans]
    return pl.pallas_call(
        functools.partial(join_kernel, plans),
        grid=(xs,),
        in_specs=[pl.BlockSpec(memory_space=pltpu.SMEM), spec, spec],
        out_specs=[pl.BlockSpec((zs * rows, out), lambda i: (i, 0)) for out in widths],
        out_shape=[jax.ShapeDtypeStruct((zs * xs * rows, out), BF16) for out in widths],
        cost_estimate=cost(6),
        compiler_params=pltpu.CompilerParams(vmem_limit_bytes=40 << 20),
    )(core_scalar(), columns, swap(columns))


def unit_plan(unit_width):
    wide = unit_width // 2
    skip = wide * 4 // 5
    return (
        (0, 0, wide),
        (1, wide - skip, wide),
        (0, wide, 2 * wide),
        (1, 2 * wide - skip, 2 * wide),
    )


def half_plan(first, width):
    half = width // 2
    return tuple(
        (core, first + side * half, first + (side + 1) * half) for side in range(2) for core in range(2)
    )


def reduce_z(grad):
    return lax.psum_scatter(grad, "z", scatter_dimension=0, tiled=True)


def reduce_z_direct(grad):
    z = lax.axis_index("z")
    parts = grad.reshape(4, -1, grad.shape[1])
    total = lax.dynamic_index_in_dim(parts, z, 0, keepdims=False).astype(F32)
    for by in range(1, 4):
        piece = lax.dynamic_index_in_dim(parts, z ^ by, 0, keepdims=False)
        total = total + flip(piece, "z", by).astype(F32)
    return total.astype(BF16)


def units_of(columns, rows):
    own = columns[0].shape[0] // XN
    unit = functools.reduce(math.gcd, [own] + [array.shape[0] for array in rows])
    half = rows[0].shape[1]
    chunk = functools.reduce(math.gcd, [half] + [array.shape[1] // 2 for array in columns])
    column_units = [
        (a, lane, part)
        for a, array in enumerate(columns)
        for lane in range(array.shape[1] // chunk)
        for part in range(own // unit)
    ]
    row_units = [
        (a, part, lane)
        for a, array in enumerate(rows)
        for part in range(array.shape[0] // unit)
        for lane in range(half // chunk)
    ]
    column_slots, row_slots = -(-len(column_units) // 4), -(-len(row_units) // 4)
    return unit, chunk, own, column_units, row_units, column_slots, row_slots


def pack_kernel(plan, column_count, *refs):
    unit, chunk, own, column_units, row_units, column_slots, row_slots = plan
    columns, rows, out = refs[:column_count], refs[column_count:-1], refs[-1]
    slots = XN * column_slots + row_slots
    for n, (a, lane, part) in enumerate(column_units):
        for x in range(XN):
            first = ((n % 4) * slots + x * column_slots + n // 4) * unit
            out[first : first + unit, :] = columns[a][
                x * own + part * unit : x * own + (part + 1) * unit,
                lane * chunk : (lane + 1) * chunk,
            ]
    for n, (a, part, lane) in enumerate(row_units):
        first = ((n % 4) * slots + XN * column_slots + n // 4) * unit
        out[first : first + unit, :] = rows[a][
            part * unit : (part + 1) * unit, lane * chunk : (lane + 1) * chunk
        ]
    empty = jnp.zeros((unit, chunk), BF16)
    for n in range(len(column_units), 4 * column_slots):
        for x in range(XN):
            first = ((n % 4) * slots + x * column_slots + n // 4) * unit
            out[first : first + unit, :] = empty
    for n in range(len(row_units), 4 * row_slots):
        first = ((n % 4) * slots + XN * column_slots + n // 4) * unit
        out[first : first + unit, :] = empty


def unpack_kernel(plan, kinds, packed, *outs):
    unit, chunk, own, column_units, row_units, column_slots, row_slots = plan
    slots = XN * column_slots + row_slots

    def block(n, c, slot):
        first = (((n % 4) * 2 + c) * slots + slot + n // 4) * unit
        return packed[first : first + unit, :].astype(F32)

    for n, (a, lane, part) in enumerate(column_units):
        kind, width, first_out = kinds[a]
        rows = slice(part * unit, (part + 1) * unit)
        for c in range(2):
            got = [block(n, c, x * column_slots) for x in range(XN)]
            if kind == "attend":
                at = c * width + lane * chunk
                query = 2 * width * 3 // 4
                for x in range(XN):
                    if at < query:
                        to = x * query + at
                        outs[first_out][rows, to : to + chunk] = got[x]
                if at >= query:
                    size = 2 * width - query
                    to = at - query
                    outs[first_out + 1][rows, to : to + chunk] = got[0] + got[2]
                    outs[first_out + 1][rows, size + to : size + to + chunk] = got[1] + got[3]
                continue
            each = width // 2
            which, at = divmod(lane * chunk, each)
            if kind == "unit":
                skip = each * 4 // 5
                quarter = each + skip
                at = at + c * skip
                if c == 1 and at < each:
                    continue
            else:
                quarter = 2 * each
                at = at + c * each
            for x in range(XN):
                to = x * quarter + at
                outs[first_out + which][rows, to : to + chunk] = got[x]
    row_outs = outs[-(1 + max(a for a, _, _ in row_units)) :]
    half = row_outs[0].shape[1] // 2
    for n, (a, part, lane) in enumerate(row_units):
        for c in range(2):
            to = c * half + lane * chunk
            row_outs[a][part * unit : (part + 1) * unit, to : to + chunk] = block(
                n, c, XN * column_slots
            )


def pack(columns, rows):
    plan = units_of(columns, rows)
    unit, chunk, _, _, _, column_slots, row_slots = plan
    return pl.pallas_call(
        functools.partial(pack_kernel, plan, len(columns)),
        out_shape=jax.ShapeDtypeStruct(
            (4 * (XN * column_slots + row_slots) * unit, chunk), BF16
        ),
        cost_estimate=cost(2),
        compiler_params=pltpu.CompilerParams(vmem_limit_bytes=40 << 20),
    )(*columns, *rows), plan


def to_owners(part, plan):
    unit, chunk, _, _, _, column_slots, row_slots = plan
    split = XN * column_slots * unit
    columns = exchange_x(part[:split].reshape(XN, column_slots * unit, chunk))
    return jnp.concatenate([columns.reshape(split, chunk), part[split:]], axis=0)


def spread(part):
    return lax.all_gather(part, ("y", "c"), axis=0, tiled=True)


def unpack(packed, plan, kinds, shapes):
    return pl.pallas_call(
        functools.partial(unpack_kernel, plan, kinds),
        out_shape=[jax.ShapeDtypeStruct(shape, F32) for shape in shapes],
        cost_estimate=cost(4),
        compiler_params=pltpu.CompilerParams(vmem_limit_bytes=48 << 20),
    )(packed)


def butterfly(value, axes):
    for axis in axes:
        by = 1
        while by < lax.axis_size(axis):
            value = value + flip(value, axis, by)
            by *= 2
    return value


def dense_forward(residual, gain, unit_weight, drop_weight):
    normed, norm_pull = jax.vjp(normalize, residual, gain)
    wide = unit_weight.shape[1] // 2
    kept = [None] * XN

    def begin(k, rows):
        return matmul(rows, unit_weight)

    def end(k, pre):
        hidden, unit_pull = jax.vjp(gated_unit, pre[:, :wide], pre[:, wide:])
        kept[k] = (hidden.astype(BF16), unit_pull)
        return matmul(kept[k][0], drop_weight)

    chunks, parts, _ = chunked(normed.astype(BF16), begin, end)
    return parts, (norm_pull, chunks, kept)


def dense_backward(residual_grad, stored, unit_weight, drop_weight, grad_chunks=None, side=()):
    norm_pull, chunks, kept = stored
    pre_grads = [None] * XN

    def begin(k, rows):
        return times_transposed(rows, drop_weight)

    def end(k, hidden_grad):
        pre_grad = kept[k][1](hidden_grad)
        pre_grads[k] = jnp.concatenate([part.astype(BF16) for part in pre_grad], axis=1)
        return times_transposed(pre_grads[k], unit_weight)

    if grad_chunks is None:
        grad_chunks, parts, side = chunked(residual_grad.astype(BF16), begin, end, side)
    else:
        parts = [None] * XN
        for k in (0, 1, 3, 2):
            parts[k] = end(k, begin(k, grad_chunks[k]))
    input_grad, gain_grad = norm_pull(scatter_chunks(parts))
    residual_grad = residual_grad + input_grad
    pre_grads, grad_chunks = after((pre_grads, grad_chunks), residual_grad)
    unit_grad = chunk_product(chunks, pre_grads, unit_pieces(unit_weight.shape[1] // 2), True)
    drop_grad = chunk_product(
        [hidden for hidden, _ in kept], grad_chunks, row_pieces(drop_weight.shape[1]), False
    )
    return residual_grad, gain_grad, unit_grad, drop_grad, side


def body(
    tokens,
    lengths,
    cotangent,
    attend_gain,
    query_weight,
    keyval_weight,
    attend_output,
    lower_gain,
    lower_gate,
    lower_lift,
    lower_drop,
    recur_gain,
    recur_input,
    recur_branch,
    recur_output,
    temporal_kernel,
    decay_gate,
    input_gate,
    decay_rate,
    upper_gain,
    upper_gate,
    upper_lift,
    upper_drop,
):
    x, z = x_index(), lax.axis_index("z")
    row_count, features = tokens.shape[1:]
    size = keyval_weight.shape[1] // 2
    query_width = query_weight.shape[1] // XN
    drop_rows, recur_rows = lower_drop.shape[0], recur_output.shape[0]
    channels = 4 * recur_rows
    tap_count = temporal_kernel.shape[0]
    even = x % 2 == 0
    members = (x + jnp.arange(XN, dtype=jnp.int32)) % XN
    positions = ((members % 2 * 4 + z) * 2 + members // 2).astype(jnp.int32)
    token_pos = positions[0] * row_count + jnp.arange(row_count, dtype=jnp.int32)
    valid = (token_pos < lengths[0]).astype(F32)[:, None]

    start_rows = tokens[0].astype(F32)
    normed_attend, attend_pull = jax.vjp(normalize, start_rows, attend_gain)
    member_query = query_weight.reshape(-1, XN, query_width).transpose(1, 0, 2)
    member_kv = jnp.stack([keyval_weight[:, (m % 2) * size : (m % 2 + 1) * size] for m in range(XN)])
    attend_columns = exchange_x(own_half(jnp.concatenate([member_query, member_kv], axis=2)))
    lower_gate, lower_lift = after((lower_gate, lower_lift), attend_columns)
    lower_columns = exchange_x(
        jnp.concatenate([unit_slices(lower_gate), unit_slices(lower_lift)], axis=2)
    )
    unit_width = lower_columns.shape[2]
    lower_rows = lax.all_gather(own_half(lower_drop), "z", axis=0, tiled=True)
    half_in = gather_direct(attend_columns).reshape(features, -1)
    attend_in = row_join(half_in)

    attend_rows = jnp.concatenate(gather_rows(normed_attend.astype(BF16)), axis=0)
    attend_rows, lower_columns = tie(attend_rows, lower_columns)
    later = (recur_input, recur_branch, upper_gate, upper_lift)
    recur_input, recur_branch, upper_gate, upper_lift = after(later, lower_columns)
    upper_columns = exchange_x(
        jnp.concatenate(
            [
                unit_slices(upper_gate),
                unit_slices(upper_lift),
                half_slices(recur_input),
                half_slices(recur_branch),
            ],
            axis=2,
        )
    )
    lower_columns = lax.all_gather(lower_columns, "z", axis=0)
    mixed_in = matmul(attend_rows, attend_in).astype(BF16).reshape(XN, row_count, -1)
    mixed_in, lower_rows, upper_columns = tie(mixed_in, lower_rows, upper_columns)
    half_out = own_half(after(attend_output, mixed_in))
    attend_out = row_join(gather_direct(half_out[None]).reshape(query_width, -1))
    queries = mixed_in[:, :, :query_width]
    kv_part = mixed_in[:, :, query_width:]
    kv_send = jnp.stack(
        [jnp.where(even, kv_part[0], kv_part[3]), jnp.where(even, kv_part[1], kv_part[0])]
    )
    kv = lax.all_to_all(
        jnp.broadcast_to(kv_send[None], (16,) + kv_send.shape), X + ("z",), 0, 0
    )
    kv, attend_out = tie(kv, attend_out)
    attended, log_total = attend_forward(positions, queries, kv)
    attend_back = attended.reshape(XN * row_count, query_width)
    parts = [matmul(attended[k], attend_out) for k in range(XN)]
    first_rows = start_rows + scatter_chunks(parts)

    lower_columns = after(lower_columns, parts)
    (lower_unit,) = column_join(lower_columns, (unit_plan(unit_width),))
    lower_down = row_join(lower_rows)
    upper_rows = own_half(jnp.concatenate([recur_output, upper_drop], axis=0))
    upper_rows = lax.all_gather(after(upper_rows, parts), "z", axis=0)
    upper_columns = lax.all_gather(upper_columns, "z", axis=0)
    upper_unit, recur_in = column_join(
        upper_columns, (unit_plan(unit_width), half_plan(unit_width, channels))
    )
    recur_out = row_join(upper_rows[:, :recur_rows].reshape(4 * recur_rows, -1))
    upper_down = row_join(upper_rows[:, recur_rows:].reshape(4 * drop_rows, -1))

    parts, lower_kept = dense_forward(first_rows, lower_gain, lower_unit, lower_down)
    second_rows = first_rows + scatter_chunks(parts)

    normed_recur, recur_pull = jax.vjp(normalize, second_rows, recur_gain)
    recur_chunks, branches, _ = chunked(
        normed_recur.astype(BF16), lambda k, rows: matmul(rows, recur_in), lambda k, branch: branch
    )
    branch_y = [part[:, channels:] for part in branches]
    x_seq = to_sequence([part[:, :channels].astype(BF16) for part in branches]).astype(F32)
    block = x * 4 + z
    width = decay_gate.shape[1]
    own_decay = lax.dynamic_slice_in_dim(decay_rate, block * width, width, 0)
    own_taps = lax.dynamic_slice_in_dim(temporal_kernel, block * width, width, 1)
    own_decay_gate = lax.dynamic_index_in_dim(decay_gate, block, 0, keepdims=False)
    own_input_gate = lax.dynamic_index_in_dim(input_gate, block, 0, keepdims=False)
    shifted = [shift_down(x_seq, k) for k in range(tap_count)]
    conv_out = sum(own_taps[k] * shifted[k] for k in range(tap_count))
    conv_low = conv_out.astype(BF16)
    pre_decay = matmul(conv_low, own_decay_gate)
    pre_admit = matmul(conv_low, own_input_gate)
    (factors, updates), gate_pull = jax.vjp(gate_terms, pre_decay, pre_admit, conv_out, own_decay)
    states = linear_scan(factors, updates, False)
    out_grad = cotangent[0].astype(F32) * valid
    out_grad_chunks = gather_rows(after(out_grad.astype(BF16), x_seq))
    states_back = from_sequence(states.astype(BF16))
    states_back, out_grad_chunks = tie(states_back, out_grad_chunks)
    merge_pulls, merged_low, parts = [], [], []
    for part, y_part in zip(states_back, branch_y):
        merged, merge_pull = jax.vjp(branch_merge, part.astype(F32), y_part)
        merge_pulls.append(merge_pull)
        merged_low.append(merged.astype(BF16))
        parts.append(matmul(merged_low[-1], recur_out))
    third_rows = second_rows + scatter_chunks(parts)

    out_parts, upper_kept = dense_forward(third_rows, upper_gain, upper_unit, upper_down)

    residual_grad, grad_upper_gain, upper_unit_grad, upper_drop_grad, _ = dense_backward(
        out_grad, upper_kept, upper_unit, upper_down, out_grad_chunks
    )
    upper_unit_grad = reduce_z(upper_unit_grad)
    upper_drop_grad = reduce_z(upper_drop_grad)

    recur_grad_chunks, merged_grads, _ = chunked(
        residual_grad.astype(BF16),
        lambda k, rows: times_transposed(rows, recur_out),
        lambda k, merged_grad: merge_pulls[k](merged_grad),
    )
    fourth_rows = third_rows + scatter_chunks(after(out_parts, merged_grads))
    out_tokens = (fourth_rows * valid).astype(BF16)[None]
    state_grad = to_sequence([part[0].astype(BF16) for part in merged_grads]).astype(F32)
    adjoint = linear_scan(shift_up(factors, 1), state_grad, True)
    decay_grad, admit_grad, conv_grad, own_decay_grad = gate_pull(
        (adjoint * shift_down(states, 1), adjoint)
    )
    decay_grad_low, admit_grad_low = decay_grad.astype(BF16), admit_grad.astype(BF16)
    conv_grad = (
        conv_grad
        + times_transposed(decay_grad_low, own_decay_gate)
        + times_transposed(admit_grad_low, own_input_gate)
    )
    own_gate_grad = transposed_times(conv_low, decay_grad_low)
    own_admit_grad = transposed_times(conv_low, admit_grad_low)
    tap_grads = jnp.stack([jnp.sum(conv_grad * shifted[k], axis=0) for k in range(tap_count)])
    x_seq_grad = sum(own_taps[k] * shift_up(conv_grad, k) for k in range(tap_count))
    channel_grads = jnp.concatenate(
        [
            own_gate_grad,
            own_admit_grad,
            tap_grads,
            own_decay_grad[None],
            jnp.zeros((3, width), F32),
        ],
        axis=0,
    )
    channel_grads = butterfly(channel_grads, ("c", "y"))
    branch_x_grad = from_sequence(x_seq_grad.astype(BF16))
    branch_x_grad, out_tokens = tie(branch_x_grad, out_tokens)
    branch_grad = [
        jnp.concatenate([x_part, part[1].astype(BF16)], axis=1)
        for x_part, part in zip(branch_x_grad, merged_grads)
    ]
    normed_grad = scatter_chunks([times_transposed(part, recur_in) for part in branch_grad])
    recur_input_grad, grad_recur_gain = recur_pull(normed_grad)
    residual_grad = residual_grad + recur_input_grad
    residual_grad, upper_unit_grad, upper_drop_grad, channel_grads = tie(
        residual_grad, upper_unit_grad, upper_drop_grad, channel_grads
    )
    branch_grad, recur_grad_chunks = after((branch_grad, recur_grad_chunks), residual_grad)
    recur_in_grad = chunk_product(recur_chunks, branch_grad, half_pieces(2 * channels), True)
    recur_out_grad = chunk_product(merged_low, recur_grad_chunks, row_pieces(features), False)
    channel_grads = lax.all_gather(channel_grads, X + ("z",), axis=0)

    residual_grad, grad_lower_gain, lower_unit_grad, lower_drop_grad, recur_grads = dense_backward(
        residual_grad, lower_kept, lower_unit, lower_down, None, (recur_in_grad, recur_out_grad)
    )
    recur_in_grad, recur_out_grad = (reduce_z(grad) for grad in recur_grads)
    residual_grad, channel_grads = tie(residual_grad, channel_grads)
    grad_chunks = gather_rows(residual_grad.astype(BF16))
    grad_chunks, lower_unit_grad, lower_drop_grad = tie(
        grad_chunks, lower_unit_grad, lower_drop_grad
    )
    grad_rows = jnp.concatenate(grad_chunks, axis=0)
    lower_unit_grad = reduce_z(lower_unit_grad)
    lower_drop_grad = reduce_z(lower_drop_grad)
    attend_grad = times_transposed(grad_rows, attend_out).astype(BF16)
    query_grad, kv_grad = attend_backward(
        positions, queries, kv, attend_grad.reshape(queries.shape), log_total
    )
    kv_grad = lax.all_to_all(kv_grad, X + ("z",), 0, 0)
    packed, upper_plan = pack([upper_unit_grad, recur_in_grad], [upper_drop_grad, recur_out_grad])
    kv_grad, query_grad, packed = tie(kv_grad, query_grad, packed)
    packed = lax.psum_scatter(packed, "y", scatter_dimension=0, tiled=True)
    upper_packed = to_owners(packed, upper_plan)
    kv_grad = jnp.sum(kv_grad.astype(F32), axis=0).astype(BF16)
    nothing = jnp.zeros_like(kv_grad[0])
    kv_grad = jnp.stack(
        [
            jnp.where(even, kv_grad[0], kv_grad[1]),
            jnp.where(even, kv_grad[1], nothing),
            nothing,
            jnp.where(even, nothing, kv_grad[0]),
        ]
    )
    mixed_grad = jnp.concatenate([query_grad, kv_grad], axis=2).reshape(XN * row_count, -1)
    normed_grad = scatter_chunks(
        [
            times_transposed(mixed_grad[k * row_count : (k + 1) * row_count], attend_in)
            for k in range(XN)
        ]
    )
    mixed_chunks = [mixed_grad[k * row_count : (k + 1) * row_count] for k in range(XN)]
    attend_chunks = [attend_rows[k * row_count : (k + 1) * row_count] for k in range(XN)]
    in_grad = reduce_z_direct(
        chunk_product(attend_chunks, mixed_chunks, row_pieces(mixed_grad.shape[1]), True)
    )
    out_grad = reduce_z_direct(
        chunk_product([attended[k] for k in range(XN)], grad_chunks, row_pieces(features), False)
    )
    packed, lower_plan = pack([lower_unit_grad, in_grad], [lower_drop_grad, out_grad])
    packed = lax.psum_scatter(packed, "y", scatter_dimension=0, tiled=True)
    packed, normed_grad, upper_packed = tie(packed, normed_grad, upper_packed)
    upper_packed = spread(upper_packed)
    lower_packed = spread(to_owners(packed, lower_plan))
    attend_input_grad, grad_attend_gain = attend_pull(normed_grad)
    residual_grad = residual_grad + attend_input_grad
    grad_decay_gate = channel_grads[:, :width]
    grad_input_gate = channel_grads[:, width : 2 * width]
    grad_temporal_kernel = (
        channel_grads[:, 2 * width : 2 * width + tap_count]
        .transpose(1, 0, 2)
        .reshape(tap_count, -1)
    )
    grad_decay_rate = channel_grads[:, 2 * width + tap_count].reshape(-1)
    gains = butterfly(
        jnp.stack([grad_attend_gain, grad_lower_gain, grad_recur_gain, grad_upper_gain]),
        ("c", "xl", "xh", "z", "y"),
    )
    upper_grads = unpack(
        upper_packed,
        upper_plan,
        (("unit", unit_width, 0), ("half", channels, 2)),
        [a.shape for a in (upper_gate, upper_lift, recur_input, recur_branch, upper_drop, recur_output)],
    )
    lower_grads = unpack(
        lower_packed,
        lower_plan,
        (("unit", unit_width, 0), ("attend", in_grad.shape[1], 2)),
        [a.shape for a in (lower_gate, lower_lift, query_weight, keyval_weight, lower_drop, attend_output)],
    )
    return (
        out_tokens,
        residual_grad[None],
        gains[0],
        *lower_grads[2:4],
        lower_grads[5],
        gains[1],
        *lower_grads[:2],
        lower_grads[4],
        gains[2],
        *upper_grads[2:4],
        upper_grads[5],
        grad_temporal_kernel,
        grad_decay_gate,
        grad_input_gate,
        grad_decay_rate,
        gains[3],
        *upper_grads[:2],
        upper_grads[4],
    )


def solution(mesh):
    grid = Mesh(mesh.devices.reshape(-1, 2, 2, 2, 4), ("y", "c", "xh", "xl", "z"))
    rows = P(("y", "c"), ("xl", "z", "xh"), None)
    weight = P(("xh", "xl", "z"), None)
    same = P()
    return jax.shard_map(
        body,
        mesh=grid,
        in_specs=(
            (rows, P(("y", "c")), rows)
            + (same, weight, weight, weight)
            + (same, weight, weight, weight)
            + (same, weight, weight, weight, same, same, same, same)
            + (same, weight, weight, weight)
        ),
        out_specs=(
            (rows, rows)
            + (same, weight, weight, weight)
            + (same, weight, weight, weight)
            + (same, weight, weight, weight, same, same, same, same)
            + (same, weight, weight, weight)
        ),
        check_vma=False,
    )
```

```python
import functools
import math

import jax
import jax.numpy as jnp
from jax import lax
from jax.experimental import pallas as pl
from jax.experimental.pallas import tpu as pltpu
from jax.sharding import Mesh, PartitionSpec as P

WINDOW = 1024
EPSILON = 1e-06
DECAY_SCALE = 8.0

X = ("xh", "xl")
XN = 4
F32 = jnp.float32
BF16 = jnp.bfloat16


def x_index():
    return lax.axis_index("xh") * 2 + lax.axis_index("xl")


def from_x(value, by):
    return lax.ppermute(value, X, [((i + by) % XN, i) for i in range(XN)])


def to_x(value, by):
    return lax.ppermute(value, X, [(i, (i + by) % XN) for i in range(XN)])


def flip(value, axis, by):
    return lax.ppermute(value, axis, [(i, i ^ by) for i in range(lax.axis_size(axis))])


def tie(main, *side):
    return lax.optimization_barrier((main, *side))


def after(value, *done):
    return lax.optimization_barrier((value, done))[0]


def swap(value):
    return lax.ppermute(value, "c", [(0, 1), (1, 0)])


def exchange_x(value):
    return lax.all_to_all(value, X, 0, 0)


def exchange_direct(value):
    x = x_index()
    out = jnp.zeros_like(value)
    for r in range(XN):
        piece = lax.dynamic_index_in_dim(value, (x + r) % XN, 0, keepdims=True)
        if r:
            piece = to_x(piece, r)
        out = lax.dynamic_update_slice_in_dim(out, piece, (x + XN - r) % XN, 0)
    return out


def by_core(mine, other):
    first = lax.axis_index("c") == 0
    return jnp.where(first, mine, other), jnp.where(first, other, mine)


def core_pick(zero, one):
    return jnp.where(lax.axis_index("c") == 0, zero, one)


def core_join(mine, other):
    return jnp.concatenate(by_core(mine, other), axis=-1)


def normalize(values, gain):
    return values * lax.rsqrt(jnp.mean(values * values, axis=-1, keepdims=True) + EPSILON) * gain


def smooth_gelu(values):
    return jax.nn.gelu(values, approximate=True)


def gated_unit(gate_pre, lift_pre):
    return smooth_gelu(gate_pre) * lift_pre


def branch_merge(states, branch_y):
    return states * smooth_gelu(branch_y)


def gate_terms(pre_decay, pre_admit, conv_out, decay_rate):
    retain = jax.nn.sigmoid(pre_decay)
    admit = jax.nn.sigmoid(pre_admit)
    log_decay = -DECAY_SCALE * jax.nn.softplus(decay_rate) * (0.25 + retain)
    return (jnp.exp(log_decay), jnp.sqrt(-jnp.expm1(2.0 * log_decay)) * admit * conv_out)


def matmul(left, right):
    return jnp.dot(left, right, preferred_element_type=F32)


def times_transposed(left, right):
    return lax.dot_general(left, right, (((1,), (1,)), ((), ())), preferred_element_type=F32)


def transposed_times(left, right):
    return lax.dot_general(left, right, (((0,), (0,)), ((), ())), preferred_element_type=F32)


def gather_rows(low):
    return [low] + [from_x(low, r) for r in range(1, XN)]


def chunked(low, begin, end, side=None):
    near = {1: from_x(low, 1), 3: from_x(low, 3)}
    first, later = tie(begin(0, low), low)
    far = from_x(later, 2)
    outs = [end(0, first)] + [None] * (XN - 1)
    extra = side((outs[0], near[1], near[3])) if side else None
    for k in (1, 3):
        outs[k] = end(k, begin(k, near[k]))
    far, outs[1], outs[3] = tie(far, outs[1], outs[3])
    outs[2] = end(2, begin(2, far))
    return [low, near[1], far, near[3]], outs, extra


def scatter_chunks(parts):
    total = parts[0]
    for r in (2, 1, 3):
        total = total + to_x(parts[r].astype(BF16), r).astype(F32)
    return total


def cost(microseconds):
    return pl.CostEstimate(flops=0, bytes_accessed=int(microseconds * 3.6e6), transcendentals=0)


def core_scalar():
    return lax.axis_index("c").astype(jnp.int32)[None]


def product_kernel(count, pieces, split, core_ref, *refs):
    lefts, rights = refs[:count], refs[count : 2 * count]
    mine_ref, other_ref, right = refs[2 * count :]
    rows = lefts[0].shape[0]

    @pl.when(pl.program_id(0) == 0)
    def _():
        for k in range(count):
            right[k * rows : (k + 1) * rows, :] = rights[k][...]

    left = jnp.concatenate([ref[...] for ref in lefts], axis=0)
    total = transposed_times(left, right[...]).astype(BF16)
    first = core_ref[0] == 0
    at = 0
    for low, high, width in pieces:
        zero, one = total[:, low : low + width], total[:, high : high + width]
        for ref, value in ((mine_ref, jnp.where(first, zero, one)), (other_ref, jnp.where(first, one, zero))):
            if split:
                each = ref.shape[2]
                for z in range(ref.shape[0]):
                    ref[z, 0, :, at : at + width] = value[z * each : (z + 1) * each]
            else:
                ref[:, at : at + width] = value
        at += width


def chunk_product(lefts, rights, pieces, split):
    rows, deep = lefts[0].shape
    width = rights[0].shape[1]
    count = len(lefts)
    kept = sum(piece[2] for piece in pieces)
    if split:
        tile = deep // XN
        shape = (4, XN, tile // 4, kept)
        spec = pl.BlockSpec((4, 1, tile // 4, kept), lambda i: (0, i, 0, 0))
    else:
        tile = next((t for t in (384, 256, 128) if deep % t == 0), deep)
        shape = (deep, kept)
        spec = pl.BlockSpec((tile, kept), lambda i: (i, 0))
    mine, other = pl.pallas_call(
        functools.partial(product_kernel, count, pieces, split),
        grid=(deep // tile,),
        in_specs=[pl.BlockSpec(memory_space=pltpu.SMEM)]
        + [pl.BlockSpec((rows, tile), lambda i: (0, i)) for _ in lefts]
        + [pl.BlockSpec((rows, width), lambda i: (0, 0)) for _ in rights],
        out_specs=[spec, spec],
        out_shape=[jax.ShapeDtypeStruct(shape, BF16)] * 2,
        scratch_shapes=[pltpu.VMEM((count * rows, width), BF16)],
        compiler_params=pltpu.CompilerParams(vmem_limit_bytes=48 << 20),
        cost_estimate=pl.CostEstimate(
            flops=2 * count * rows * deep * width,
            bytes_accessed=2 * (count * rows * (deep + width) + 2 * deep * kept),
            transcendentals=0,
        ),
    )(core_scalar(), *lefts, *rights)
    total = (mine.astype(F32) + swap(other).astype(F32)).astype(BF16)
    return total.reshape(-1, kept)


def unit_pieces(quarter):
    wide = quarter * 5 // 9
    return ((0, quarter - wide, wide), (quarter, 2 * quarter - wide, wide))


def half_pieces(width):
    half = width // 4
    return ((0, half, half), (2 * half, 3 * half, half))


def row_pieces(width):
    return ((0, width // 2, width // 2),)


def kv_places(rows):
    places = []
    for x in range(XN):
        for z in range(4):
            for j in range(2):
                position = (j * 4 + z) * 2 + x // 2
                places.append((x * 4 + z, j, x % 2, WINDOW + position * rows))
    return places


def attend_scores(pos_ref, q_ref, key_s, scale):
    rows, size = q_ref.shape[1], key_s.shape[1]
    heads = q_ref.shape[2] // size
    start = pl.multiple_of(pos_ref[pl.program_id(0)] * rows, rows)
    query = q_ref[0]
    query = jnp.concatenate([query[:, h * size : (h + 1) * size] for h in range(heads)], axis=0)
    key = key_s[pl.ds(start, WINDOW + rows), :]
    scores = times_transposed(query, key) * scale
    row = lax.broadcasted_iota(jnp.int32, scores.shape, 0) % rows
    col = lax.broadcasted_iota(jnp.int32, scores.shape, 1)
    allowed = (col > row) & (col <= row + WINDOW) & (col >= WINDOW - start)
    return start, query, key, jnp.where(allowed, scores, -1e30)


def load_kv(kv_ref, key_s, value_s):
    rows = kv_ref.shape[2]
    key_s[:WINDOW, :] = jnp.zeros((WINDOW, key_s.shape[1]), key_s.dtype)
    value_s[:WINDOW, :] = jnp.zeros((WINDOW, key_s.shape[1]), key_s.dtype)
    for source, j, kind, first in kv_places(rows):
        (value_s if kind else key_s)[first : first + rows, :] = kv_ref[source, j]


def attend_forward_kernel(scale, pos_ref, q_ref, kv_ref, out_ref, lse_ref, key_s, value_s):
    rows, size = q_ref.shape[1], key_s.shape[1]

    @pl.when(pl.program_id(0) == 0)
    def _():
        load_kv(kv_ref, key_s, value_s)

    start, query, key, scores = attend_scores(pos_ref, q_ref, key_s, scale)
    highest = jnp.max(scores, axis=-1, keepdims=True)
    lse = highest + jnp.log(jnp.sum(jnp.exp(scores - highest), axis=-1, keepdims=True))
    probs = jnp.exp(scores - lse).astype(BF16)
    mixed = matmul(probs, value_s[pl.ds(start, WINDOW + rows), :]).astype(BF16)
    out_ref[0] = jnp.concatenate(
        [mixed[h * rows : (h + 1) * rows] for h in range(q_ref.shape[2] // size)], axis=1
    )
    lse_ref[0] = lse


def attend_backward_kernel(
    scale, pos_ref, q_ref, kv_ref, grad_ref, lse_ref, dq_ref, dkv_ref, key_s, value_s, dk_s, dv_s
):
    rows, size = q_ref.shape[1], key_s.shape[1]
    heads = q_ref.shape[2] // size

    @pl.when(pl.program_id(0) == 0)
    def _():
        load_kv(kv_ref, key_s, value_s)
        dk_s[...] = jnp.zeros_like(dk_s)
        dv_s[...] = jnp.zeros_like(dv_s)

    start, query, key, scores = attend_scores(pos_ref, q_ref, key_s, scale)
    span = pl.ds(start, WINDOW + rows)
    probs = jnp.exp(scores - lse_ref[0])
    grad = grad_ref[0]
    grad = jnp.concatenate([grad[:, h * size : (h + 1) * size] for h in range(heads)], axis=0)
    prob_grad = times_transposed(grad, value_s[span, :])
    delta = jnp.sum(probs * prob_grad, axis=-1, keepdims=True)
    score_grad = (probs * (prob_grad - delta)).astype(BF16)
    query_grad = (matmul(score_grad, key) * scale).astype(BF16)
    dq_ref[0] = jnp.concatenate(
        [query_grad[h * rows : (h + 1) * rows] for h in range(heads)], axis=1
    )
    dk_s[span, :] += transposed_times(score_grad, query) * scale
    dv_s[span, :] += transposed_times(probs.astype(BF16), grad)

    @pl.when(pl.program_id(0) == pl.num_programs(0) - 1)
    def _():
        for source, j, kind, first in kv_places(rows):
            dkv_ref[source, j] = (dv_s if kind else dk_s)[first : first + rows, :].astype(BF16)


def whole(array):
    return pl.BlockSpec(array.shape, lambda r: (0,) * len(array.shape))


def by_block(*shape):
    return pl.BlockSpec((1,) + shape, lambda r: (r, 0, 0))


def kv_scratch(kv, dtype):
    return pltpu.VMEM((WINDOW + 16 * kv.shape[2], kv.shape[3]), dtype)


def attend_forward(positions, query, kv):
    blocks, rows, width = query.shape
    size = kv.shape[3]
    stacked = rows * (width // size)
    return pl.pallas_call(
        functools.partial(attend_forward_kernel, size**-0.5),
        grid=(blocks,),
        in_specs=[pl.BlockSpec(memory_space=pltpu.SMEM), by_block(rows, width), whole(kv)],
        out_specs=[by_block(rows, width), by_block(stacked, 1)],
        out_shape=[
            jax.ShapeDtypeStruct(query.shape, BF16),
            jax.ShapeDtypeStruct((blocks, stacked, 1), F32),
        ],
        scratch_shapes=[kv_scratch(kv, BF16), kv_scratch(kv, BF16)],
        cost_estimate=cost(7),
        compiler_params=pltpu.CompilerParams(vmem_limit_bytes=40 << 20),
    )(positions, query, kv)


def attend_backward(positions, query, kv, grad, lse):
    blocks, rows, width = query.shape
    size = kv.shape[3]
    stacked = rows * (width // size)
    return pl.pallas_call(
        functools.partial(attend_backward_kernel, size**-0.5),
        grid=(blocks,),
        in_specs=[
            pl.BlockSpec(memory_space=pltpu.SMEM),
            by_block(rows, width),
            whole(kv),
            by_block(rows, width),
            by_block(stacked, 1),
        ],
        out_specs=[by_block(rows, width), whole(kv)],
        out_shape=[
            jax.ShapeDtypeStruct(query.shape, BF16),
            jax.ShapeDtypeStruct(kv.shape, BF16),
        ],
        scratch_shapes=[
            kv_scratch(kv, BF16),
            kv_scratch(kv, BF16),
            kv_scratch(kv, F32),
            kv_scratch(kv, F32),
        ],
        cost_estimate=cost(9),
        compiler_params=pltpu.CompilerParams(vmem_limit_bytes=40 << 20),
    )(positions, query, kv, grad, lse)


def scan_kernel(backward, factor_ref, update_ref, state_ref):
    tiles = factor_ref.shape[0] // 8
    width = factor_ref.shape[1]
    row = lax.broadcasted_iota(jnp.int32, (8, width), 0)

    def turn(index, carry):
        tile = tiles - 1 - index if backward else index
        span = pl.ds(pl.multiple_of(tile * 8, 8), 8)
        factor, update = factor_ref[span, :], update_ref[span, :]
        for reach in (1, 2, 4):
            shift = 8 - reach if backward else reach
            inside = row < 8 - reach if backward else row >= reach
            far_update = pltpu.roll(update, shift, 0)
            far_factor = pltpu.roll(factor, shift, 0)
            update = jnp.where(inside, factor * far_update + update, update)
            factor = jnp.where(inside, factor * far_factor, factor)
        state = factor * carry + update
        state_ref[span, :] = state
        last = state[0:1] if backward else state[7:8]
        return jnp.broadcast_to(last, (8, width))

    lax.fori_loop(0, tiles, turn, jnp.zeros((8, width), F32), unroll=8)


def linear_scan(factors, updates, backward):
    return pl.pallas_call(
        functools.partial(scan_kernel, backward),
        out_shape=jax.ShapeDtypeStruct(factors.shape, F32),
        cost_estimate=cost(1.5),
        compiler_params=pltpu.CompilerParams(vmem_limit_bytes=24 << 20),
    )(factors, updates)


def to_sequence(chunks):
    rows, width = chunks[0].shape[0], chunks[0].shape[1] // 4
    sent = jnp.stack(
        [jnp.stack([part[:, b * width : (b + 1) * width] for part in chunks]) for b in range(4)]
    )
    got = lax.all_to_all(sent, "z", 0, 0)
    got = jnp.roll(got, x_index(), axis=1).reshape(4, 2, 2, rows, width)
    return got.transpose(2, 0, 1, 3, 4).reshape(16 * rows, width)


def from_sequence(values):
    rows, width = values.shape[0] // 16, values.shape[1]
    sent = values.reshape(2, 4, 2, rows, width).transpose(1, 2, 0, 3, 4)
    sent = jnp.roll(sent.reshape(4, XN, rows, width), -x_index(), axis=1)
    got = lax.all_to_all(sent, "z", 0, 0)
    return [jnp.concatenate([got[b, k] for b in range(4)], axis=1) for k in range(XN)]


def shift_down(values, by):
    if by == 0:
        return values
    return jnp.concatenate([jnp.zeros_like(values[:by]), values[:-by]], axis=0)


def shift_up(values, by):
    if by == 0:
        return values
    return jnp.concatenate([values[by:], jnp.zeros_like(values[:by])], axis=0)


def unit_slices(weight):
    quarter = weight.shape[1] // XN
    wide = quarter * 5 // 9
    skip = quarter - wide
    keep = lax.broadcasted_iota(jnp.int32, (weight.shape[0], wide), 1) >= wide - skip
    picked = []
    for member in range(XN):
        columns = weight[:, member * quarter : (member + 1) * quarter]
        picked.append(core_pick(columns[:, :wide], jnp.where(keep, columns[:, skip:], 0)))
    return jnp.stack(picked)


def half_slices(weight):
    quarter = weight.shape[1] // XN
    half = quarter // 2
    picked = []
    for member in range(XN):
        columns = weight[:, member * quarter : (member + 1) * quarter]
        picked.append(core_pick(columns[:, :half], columns[:, half:]))
    return jnp.stack(picked)


def own_half(weight):
    half = weight.shape[-1] // 2
    return core_pick(weight[..., :half], weight[..., half:])


def other_half(weight):
    half = weight.shape[-1] // 2
    return core_pick(weight[..., half:], weight[..., :half])


def gather_direct(value):
    z = lax.axis_index("z")
    out = jnp.zeros((value.shape[0], 4) + value.shape[1:], value.dtype)
    for by in range(4):
        piece = flip(value, "z", by) if by else value
        out = lax.dynamic_update_slice_in_dim(out, piece[:, None], z ^ by, 1)
    return out


def row_join(rows):
    return core_join(rows, swap(rows))


def join_kernel(plans, core_ref, mine_ref, other_ref, *outs):
    first = core_ref[0] == 0
    each = mine_ref.shape[2]
    for z in range(mine_ref.shape[0]):
        mine, other = mine_ref[z, 0], other_ref[z, 0]
        zero, one = jnp.where(first, mine, other), jnp.where(first, other, mine)
        for out, pieces in zip(outs, plans):
            at = 0
            for core, low, high in pieces:
                out[z * each : (z + 1) * each, at : at + high - low] = (one if core else zero)[:, low:high]
                at += high - low


def column_join(columns, plans):
    zs, xs, rows, width = columns.shape
    spec = pl.BlockSpec((zs, 1, rows, width), lambda i: (0, i, 0, 0))
    widths = [sum(high - low for _, low, high in pieces) for pieces in plans]
    return pl.pallas_call(
        functools.partial(join_kernel, plans),
        grid=(xs,),
        in_specs=[pl.BlockSpec(memory_space=pltpu.SMEM), spec, spec],
        out_specs=[pl.BlockSpec((zs * rows, out), lambda i: (i, 0)) for out in widths],
        out_shape=[jax.ShapeDtypeStruct((zs * xs * rows, out), BF16) for out in widths],
        cost_estimate=cost(6),
        compiler_params=pltpu.CompilerParams(vmem_limit_bytes=40 << 20),
    )(core_scalar(), columns, swap(columns))


def unit_plan(unit_width):
    wide = unit_width // 2
    skip = wide * 4 // 5
    return (
        (0, 0, wide),
        (1, wide - skip, wide),
        (0, wide, 2 * wide),
        (1, 2 * wide - skip, 2 * wide),
    )


def half_plan(first, width):
    half = width // 2
    return tuple(
        (core, first + side * half, first + (side + 1) * half) for side in range(2) for core in range(2)
    )


def reduce_z(grad):
    return lax.psum_scatter(grad, "z", scatter_dimension=0, tiled=True)


def reduce_direct(grad, axis):
    at = lax.axis_index(axis)
    parts = grad.reshape(4, -1, grad.shape[1])
    total = lax.dynamic_index_in_dim(parts, at, 0, keepdims=False).astype(F32)
    for by in (2, 1, 3):
        piece = lax.dynamic_index_in_dim(parts, at ^ by, 0, keepdims=False)
        total = total + flip(piece, axis, by).astype(F32)
    return total.astype(BF16)


def units_of(columns, rows):
    own = columns[0].shape[0] // XN
    unit = functools.reduce(math.gcd, [own] + [array.shape[0] for array in rows])
    half = rows[0].shape[1]
    chunk = functools.reduce(math.gcd, [half] + [array.shape[1] // 2 for array in columns])
    column_units = [
        (a, lane, part)
        for a, array in enumerate(columns)
        for lane in range(array.shape[1] // chunk)
        for part in range(own // unit)
    ]
    row_units = [
        (a, part, lane)
        for a, array in enumerate(rows)
        for part in range(array.shape[0] // unit)
        for lane in range(half // chunk)
    ]
    column_slots, row_slots = -(-len(column_units) // 4), -(-len(row_units) // 4)
    return unit, chunk, own, column_units, row_units, column_slots, row_slots


def pack_kernel(plan, column_count, *refs):
    unit, chunk, own, column_units, row_units, column_slots, row_slots = plan
    columns, rows, out = refs[:column_count], refs[column_count:-1], refs[-1]
    slots = XN * column_slots + row_slots
    for n, (a, lane, part) in enumerate(column_units):
        for x in range(XN):
            first = ((n % 4) * slots + x * column_slots + n // 4) * unit
            out[first : first + unit, :] = columns[a][
                x * own + part * unit : x * own + (part + 1) * unit,
                lane * chunk : (lane + 1) * chunk,
            ]
    for n, (a, part, lane) in enumerate(row_units):
        first = ((n % 4) * slots + XN * column_slots + n // 4) * unit
        out[first : first + unit, :] = rows[a][
            part * unit : (part + 1) * unit, lane * chunk : (lane + 1) * chunk
        ]
    empty = jnp.zeros((unit, chunk), BF16)
    for n in range(len(column_units), 4 * column_slots):
        for x in range(XN):
            first = ((n % 4) * slots + x * column_slots + n // 4) * unit
            out[first : first + unit, :] = empty
    for n in range(len(row_units), 4 * row_slots):
        first = ((n % 4) * slots + XN * column_slots + n // 4) * unit
        out[first : first + unit, :] = empty


def unpack_kernel(plan, kinds, packed, *outs):
    unit, chunk, own, column_units, row_units, column_slots, row_slots = plan
    slots = XN * column_slots + row_slots

    def block(n, c, slot):
        first = (((n % 4) * 2 + c) * slots + slot + n // 4) * unit
        return packed[first : first + unit, :].astype(F32)

    for n, (a, lane, part) in enumerate(column_units):
        kind, width, first_out = kinds[a]
        rows = slice(part * unit, (part + 1) * unit)
        for c in range(2):
            got = [block(n, c, x * column_slots) for x in range(XN)]
            if kind == "attend":
                at = c * width + lane * chunk
                query = 2 * width * 3 // 4
                for x in range(XN):
                    if at < query:
                        to = x * query + at
                        outs[first_out][rows, to : to + chunk] = got[x]
                if at >= query:
                    size = 2 * width - query
                    to = at - query
                    outs[first_out + 1][rows, to : to + chunk] = got[0] + got[2]
                    outs[first_out + 1][rows, size + to : size + to + chunk] = got[1] + got[3]
                continue
            each = width // 2
            which, at = divmod(lane * chunk, each)
            if kind == "unit":
                skip = each * 4 // 5
                quarter = each + skip
                at = at + c * skip
                if c == 1 and at < each:
                    continue
            else:
                quarter = 2 * each
                at = at + c * each
            for x in range(XN):
                to = x * quarter + at
                outs[first_out + which][rows, to : to + chunk] = got[x]
    row_outs = outs[-(1 + max(a for a, _, _ in row_units)) :]
    half = row_outs[0].shape[1] // 2
    for n, (a, part, lane) in enumerate(row_units):
        for c in range(2):
            to = c * half + lane * chunk
            row_outs[a][part * unit : (part + 1) * unit, to : to + chunk] = block(
                n, c, XN * column_slots
            )


def pack(columns, rows):
    plan = units_of(columns, rows)
    unit, chunk, _, _, _, column_slots, row_slots = plan
    return pl.pallas_call(
        functools.partial(pack_kernel, plan, len(columns)),
        out_shape=jax.ShapeDtypeStruct(
            (4 * (XN * column_slots + row_slots) * unit, chunk), BF16
        ),
        cost_estimate=cost(2),
        compiler_params=pltpu.CompilerParams(vmem_limit_bytes=40 << 20),
    )(*columns, *rows), plan


def to_owners(part, plan):
    unit, chunk, _, _, _, column_slots, row_slots = plan
    split = XN * column_slots * unit
    columns = exchange_x(part[:split].reshape(XN, column_slots * unit, chunk))
    return jnp.concatenate([columns.reshape(split, chunk), part[split:]], axis=0)


def spread(part):
    return lax.all_gather(part, ("y", "c"), axis=0, tiled=True)


def spread_direct(part):
    y = lax.axis_index("y")
    out = jnp.zeros((4,) + part.shape, part.dtype)
    for by in range(4):
        piece = flip(part, "y", by) if by else part
        out = lax.dynamic_update_slice_in_dim(out, piece[None], y ^ by, 0)
    return jnp.stack(by_core(out, swap(out)), axis=1).reshape(-1, part.shape[1])


def unpack(packed, plan, kinds, shapes):
    return pl.pallas_call(
        functools.partial(unpack_kernel, plan, kinds),
        out_shape=[jax.ShapeDtypeStruct(shape, F32) for shape in shapes],
        cost_estimate=cost(4),
        compiler_params=pltpu.CompilerParams(vmem_limit_bytes=48 << 20),
    )(packed)


def butterfly(value, axes):
    for axis in axes:
        by = 1
        while by < lax.axis_size(axis):
            value = value + flip(value, axis, by)
            by *= 2
    return value


def dense_forward(residual, gain, unit_weight, drop_weight):
    normed, norm_pull = jax.vjp(normalize, residual, gain)
    wide = unit_weight.shape[1] // 2
    kept = [None] * XN

    def begin(k, rows):
        return matmul(rows, unit_weight)

    def end(k, pre):
        hidden, unit_pull = jax.vjp(gated_unit, pre[:, :wide], pre[:, wide:])
        kept[k] = (hidden.astype(BF16), unit_pull)
        return matmul(kept[k][0], drop_weight)

    chunks, parts, _ = chunked(normed.astype(BF16), begin, end)
    return parts, (norm_pull, chunks, kept)


def dense_backward(residual_grad, stored, unit_weight, drop_weight, grad_chunks=None, side=None):
    norm_pull, chunks, kept = stored
    pre_grads = [None] * XN

    def begin(k, rows):
        return times_transposed(rows, drop_weight)

    def end(k, hidden_grad):
        pre_grad = kept[k][1](hidden_grad)
        pre_grads[k] = jnp.concatenate([part.astype(BF16) for part in pre_grad], axis=1)
        return times_transposed(pre_grads[k], unit_weight)

    extra = None
    if grad_chunks is None:
        grad_chunks, parts, extra = chunked(residual_grad.astype(BF16), begin, end, side)
    else:
        parts = [None] * XN
        for k in (0, 1, 3, 2):
            parts[k] = end(k, begin(k, grad_chunks[k]))
    input_grad, gain_grad = norm_pull(scatter_chunks(parts))

    def products(done):
        pre, grads = after((pre_grads, grad_chunks), done)
        return (
            chunk_product(chunks, pre, unit_pieces(unit_weight.shape[1] // 2), True),
            chunk_product(
                [hidden for hidden, _ in kept], grads, row_pieces(drop_weight.shape[1]), False
            ),
        )

    return residual_grad + input_grad, gain_grad, products, extra


def body(
    tokens,
    lengths,
    cotangent,
    attend_gain,
    query_weight,
    keyval_weight,
    attend_output,
    lower_gain,
    lower_gate,
    lower_lift,
    lower_drop,
    recur_gain,
    recur_input,
    recur_branch,
    recur_output,
    temporal_kernel,
    decay_gate,
    input_gate,
    decay_rate,
    upper_gain,
    upper_gate,
    upper_lift,
    upper_drop,
):
    x, z = x_index(), lax.axis_index("z")
    row_count, features = tokens.shape[1:]
    size = keyval_weight.shape[1] // 2
    query_width = query_weight.shape[1] // XN
    drop_rows, recur_rows = lower_drop.shape[0], recur_output.shape[0]
    channels = 4 * recur_rows
    tap_count = temporal_kernel.shape[0]
    even = x % 2 == 0
    members = (x + jnp.arange(XN, dtype=jnp.int32)) % XN
    positions = ((members % 2 * 4 + z) * 2 + members // 2).astype(jnp.int32)
    token_pos = positions[0] * row_count + jnp.arange(row_count, dtype=jnp.int32)
    valid = (token_pos < lengths[0]).astype(F32)[:, None]

    start_rows = tokens[0].astype(F32)
    normed_attend, attend_pull = jax.vjp(normalize, start_rows, attend_gain)
    member_query = query_weight.reshape(-1, XN, query_width).transpose(1, 0, 2)
    member_kv = jnp.stack([keyval_weight[:, (m % 2) * size : (m % 2 + 1) * size] for m in range(XN)])
    lower_columns = exchange_x(
        jnp.concatenate([unit_slices(lower_gate), unit_slices(lower_lift)], axis=2)
    )
    unit_width = lower_columns.shape[2]
    attend_columns = own_half(jnp.concatenate([member_query, member_kv], axis=2))
    half_in = lax.all_to_all(jnp.repeat(attend_columns, 4, axis=0), X + ("z",), 0, 0)
    attend_in = row_join(half_in.reshape(features, -1))
    half_out = gather_direct(own_half(attend_output)[None])
    lower_rows = lax.all_gather(own_half(lower_drop), "z", axis=0, tiled=True)

    attend_rows = jnp.concatenate(gather_rows(normed_attend.astype(BF16)), axis=0)
    attend_rows, attend_in, lower_columns, lower_rows, half_out = tie(
        attend_rows, attend_in, lower_columns, lower_rows, half_out
    )
    lower_columns = lax.all_gather(lower_columns, "z", axis=0)
    recur_input, recur_branch, upper_gate, upper_lift = after(
        (recur_input, recur_branch, upper_gate, upper_lift), attend_rows
    )
    upper_columns = exchange_direct(
        jnp.concatenate(
            [
                half_slices(recur_input),
                half_slices(recur_branch),
                unit_slices(upper_gate),
                unit_slices(upper_lift),
            ],
            axis=2,
        )
    )
    mixed_in = matmul(attend_rows, attend_in).astype(BF16).reshape(XN, row_count, -1)
    attend_out = row_join(half_out.reshape(query_width, -1))
    queries = mixed_in[:, :, :query_width]
    kv_part = mixed_in[:, :, query_width:]
    kv_send = jnp.stack(
        [jnp.where(even, kv_part[0], kv_part[3]), jnp.where(even, kv_part[1], kv_part[0])]
    )
    kv = lax.all_to_all(
        jnp.broadcast_to(kv_send[None], (16,) + kv_send.shape), X + ("z",), 0, 0
    )
    out_grad = cotangent[0].astype(F32) * valid
    out_grad_chunks = gather_rows(after(out_grad.astype(BF16), kv))
    attended, log_total = attend_forward(positions, queries, kv)
    attended, out_grad_chunks = tie(attended, out_grad_chunks)
    attend_back = attended.reshape(XN * row_count, query_width)
    parts = [matmul(attended[k], attend_out) for k in range(XN)]
    first_rows = start_rows + scatter_chunks(parts)
    first_rows, upper_columns = tie(first_rows, upper_columns)

    lower_columns, lower_rows = after((lower_columns, lower_rows), first_rows)
    (lower_unit,) = column_join(lower_columns, (unit_plan(unit_width),))
    lower_down = row_join(lower_rows)
    recur_columns = lax.all_gather(upper_columns[:, :, :channels], "z", axis=0)
    upper_rows = own_half(jnp.concatenate([recur_output, upper_drop], axis=0))
    upper_rows = lax.all_gather(after(upper_rows, parts), "z", axis=0)
    upper_columns = lax.all_gather(after(upper_columns, parts)[:, :, channels:], "z", axis=0)

    parts, lower_kept = dense_forward(first_rows, lower_gain, lower_unit, lower_down)
    second_rows = first_rows + scatter_chunks(parts)
    recur_columns, upper_rows = after((recur_columns, upper_rows), second_rows)
    (recur_in,) = column_join(recur_columns, (half_plan(0, channels),))
    recur_out = row_join(upper_rows[:, :recur_rows].reshape(4 * recur_rows, -1))

    normed_recur, recur_pull = jax.vjp(normalize, second_rows, recur_gain)
    recur_chunks, branches, _ = chunked(
        normed_recur.astype(BF16), lambda k, rows: matmul(rows, recur_in), lambda k, branch: branch
    )
    branch_y = [part[:, channels:] for part in branches]
    x_seq = to_sequence([part[:, :channels].astype(BF16) for part in branches]).astype(F32)
    upper_columns, upper_rows = after((upper_columns, upper_rows), branches)
    (upper_unit,) = column_join(upper_columns, (unit_plan(unit_width),))
    upper_down = row_join(upper_rows[:, recur_rows:].reshape(4 * drop_rows, -1))
    block = x * 4 + z
    width = decay_gate.shape[1]
    own_decay = lax.dynamic_slice_in_dim(decay_rate, block * width, width, 0)
    own_taps = lax.dynamic_slice_in_dim(temporal_kernel, block * width, width, 1)
    own_decay_gate = lax.dynamic_index_in_dim(decay_gate, block, 0, keepdims=False)
    own_input_gate = lax.dynamic_index_in_dim(input_gate, block, 0, keepdims=False)
    shifted = [shift_down(x_seq, k) for k in range(tap_count)]
    conv_out = sum(own_taps[k] * shifted[k] for k in range(tap_count))
    conv_low = conv_out.astype(BF16)
    pre_decay = matmul(conv_low, own_decay_gate)
    pre_admit = matmul(conv_low, own_input_gate)
    (factors, updates), gate_pull = jax.vjp(gate_terms, pre_decay, pre_admit, conv_out, own_decay)
    states = linear_scan(factors, updates, False)
    states_back = from_sequence(states.astype(BF16))
    merge_pulls, merged_low, parts = [], [], []
    for part, y_part in zip(states_back, branch_y):
        merged, merge_pull = jax.vjp(branch_merge, part.astype(F32), y_part)
        merge_pulls.append(merge_pull)
        merged_low.append(merged.astype(BF16))
        parts.append(matmul(merged_low[-1], recur_out))
    third_rows = second_rows + scatter_chunks(parts)

    out_parts, upper_kept = dense_forward(third_rows, upper_gain, upper_unit, upper_down)

    residual_grad, grad_upper_gain, upper_products, _ = dense_backward(
        out_grad, upper_kept, upper_unit, upper_down, out_grad_chunks
    )
    recur_grad_chunks, merged_grads, upper_grads = chunked(
        residual_grad.astype(BF16),
        lambda k, rows: times_transposed(rows, recur_out),
        lambda k, merged_grad: merge_pulls[k](merged_grad),
        upper_products,
    )
    fourth_rows = third_rows + scatter_chunks(after(out_parts, merged_grads))
    out_tokens = (fourth_rows * valid).astype(BF16)[None]
    state_grad = to_sequence([part[0].astype(BF16) for part in merged_grads]).astype(F32)
    adjoint = linear_scan(shift_up(factors, 1), state_grad, True)
    decay_grad, admit_grad, conv_grad, own_decay_grad = gate_pull(
        (adjoint * shift_down(states, 1), adjoint)
    )
    decay_grad_low, admit_grad_low = decay_grad.astype(BF16), admit_grad.astype(BF16)
    conv_grad = (
        conv_grad
        + times_transposed(decay_grad_low, own_decay_gate)
        + times_transposed(admit_grad_low, own_input_gate)
    )
    own_gate_grad = transposed_times(conv_low, decay_grad_low)
    own_admit_grad = transposed_times(conv_low, admit_grad_low)
    tap_grads = jnp.stack([jnp.sum(conv_grad * shifted[k], axis=0) for k in range(tap_count)])
    x_seq_grad = sum(own_taps[k] * shift_up(conv_grad, k) for k in range(tap_count))
    channel_grads = jnp.concatenate(
        [
            own_gate_grad,
            own_admit_grad,
            tap_grads,
            own_decay_grad[None],
            jnp.zeros((3, width), F32),
        ],
        axis=0,
    )
    branch_x_grad = from_sequence(x_seq_grad.astype(BF16))
    branch_x_grad, out_tokens = tie(branch_x_grad, out_tokens)
    branch_grad = [
        jnp.concatenate([x_part, part[1].astype(BF16)], axis=1)
        for x_part, part in zip(branch_x_grad, merged_grads)
    ]
    normed_grad = scatter_chunks([times_transposed(part, recur_in) for part in branch_grad])
    recur_input_grad, grad_recur_gain = recur_pull(normed_grad)
    residual_grad = residual_grad + recur_input_grad
    residual_grad, upper_grads = tie(residual_grad, upper_grads)
    upper_unit_grad, upper_drop_grad = (reduce_z(grad) for grad in upper_grads)

    def recur_products(done):
        branch, grads = after((branch_grad, recur_grad_chunks), done)
        return (
            chunk_product(recur_chunks, branch, half_pieces(2 * channels), True),
            chunk_product(merged_low, grads, row_pieces(features), False),
        )

    residual_grad, grad_lower_gain, lower_products, recur_grads = dense_backward(
        residual_grad, lower_kept, lower_unit, lower_down, None, recur_products
    )
    residual_grad, recur_grads, upper_drop_grad = tie(
        residual_grad, recur_grads, upper_drop_grad
    )
    recur_in_grad, recur_out_grad = (reduce_z(grad) for grad in recur_grads)
    grad_chunks, attend_grad, lower_grads = chunked(
        residual_grad.astype(BF16),
        lambda k, rows: times_transposed(rows, attend_out).astype(BF16),
        lambda k, grad: grad,
        lambda done: lower_products((done, upper_unit_grad)),
    )
    attend_grad = jnp.stack(attend_grad)
    query_grad, kv_grad = attend_backward(
        positions, queries, kv, attend_grad, log_total
    )
    kv_grad = lax.all_to_all(kv_grad, X + ("z",), 0, 0)
    out_grad = chunk_product(
        [attended[k] for k in range(XN)], grad_chunks, row_pieces(features), False
    )
    kv_grad, query_grad, out_grad, lower_grads = tie(kv_grad, query_grad, out_grad, lower_grads)
    lower_unit_grad, lower_drop_grad = (reduce_z(grad) for grad in lower_grads)
    kv_grad = jnp.sum(kv_grad.astype(F32), axis=0).astype(BF16)
    nothing = jnp.zeros_like(kv_grad[0])
    kv_grad = jnp.stack(
        [
            jnp.where(even, kv_grad[0], kv_grad[1]),
            jnp.where(even, kv_grad[1], nothing),
            nothing,
            jnp.where(even, nothing, kv_grad[0]),
        ]
    )
    mixed_grad = jnp.concatenate([query_grad, kv_grad], axis=2).reshape(XN * row_count, -1)
    mixed_chunks = [mixed_grad[k * row_count : (k + 1) * row_count] for k in range(XN)]
    attend_chunks = [attend_rows[k * row_count : (k + 1) * row_count] for k in range(XN)]
    in_grad = chunk_product(attend_chunks, mixed_chunks, row_pieces(mixed_grad.shape[1]), True)
    lanes = in_grad.shape[1]
    out_rows = out_grad.reshape(4, -1, features // 2)
    both = [in_grad.reshape(4, -1, lanes)]
    both += [out_rows[:, :, at : at + lanes] for at in range(0, features // 2, lanes)]
    both = reduce_direct(jnp.concatenate(both, axis=1).reshape(-1, lanes), "z")
    normed_grad = scatter_chunks(
        [times_transposed(part, attend_in) for part in after(mixed_chunks, in_grad)]
    )
    channel_grads = butterfly(after(channel_grads, kv_grad), ("c", "y"))
    both, normed_grad, channel_grads = tie(both, normed_grad, channel_grads)
    recur_in_grad, recur_out_grad = after((recur_in_grad, recur_out_grad), both)
    packed, upper_plan = pack([upper_unit_grad, recur_in_grad], [upper_drop_grad, recur_out_grad])
    channel_grads = lax.all_to_all(
        jnp.broadcast_to(channel_grads, (16,) + channel_grads.shape), X + ("z",), 0, 0
    )
    packed, channel_grads = tie(reduce_direct(packed, "y"), channel_grads)
    upper_packed = spread(to_owners(packed, upper_plan))
    in_grad, out_grad = both[: features // 4], both[features // 4 :].reshape(-1, features // 16, lanes)
    out_grad = jnp.concatenate([out_grad[k] for k in range(out_grad.shape[0])], axis=1)
    packed, lower_plan = pack([lower_unit_grad, in_grad], [lower_drop_grad, out_grad])
    packed, upper_packed = tie(reduce_direct(packed, "y"), upper_packed)
    lower_packed = spread(to_owners(packed, lower_plan))
    attend_input_grad, grad_attend_gain = attend_pull(normed_grad)
    gains = butterfly(
        jnp.stack([grad_attend_gain, grad_lower_gain, grad_recur_gain, grad_upper_gain]),
        ("c", "xl", "xh", "z", "y"),
    )
    residual_grad = residual_grad + attend_input_grad
    grad_decay_gate = channel_grads[:, :width]
    grad_input_gate = channel_grads[:, width : 2 * width]
    grad_temporal_kernel = (
        channel_grads[:, 2 * width : 2 * width + tap_count]
        .transpose(1, 0, 2)
        .reshape(tap_count, -1)
    )
    grad_decay_rate = channel_grads[:, 2 * width + tap_count].reshape(-1)
    upper_grads = unpack(
        upper_packed,
        upper_plan,
        (("unit", unit_width, 0), ("half", channels, 2)),
        [a.shape for a in (upper_gate, upper_lift, recur_input, recur_branch, upper_drop, recur_output)],
    )
    lower_grads = unpack(
        lower_packed,
        lower_plan,
        (("unit", unit_width, 0), ("attend", in_grad.shape[1], 2)),
        [a.shape for a in (lower_gate, lower_lift, query_weight, keyval_weight, lower_drop, attend_output)],
    )
    return (
        out_tokens,
        residual_grad[None],
        gains[0],
        *lower_grads[2:4],
        lower_grads[5],
        gains[1],
        *lower_grads[:2],
        lower_grads[4],
        gains[2],
        *upper_grads[2:4],
        upper_grads[5],
        grad_temporal_kernel,
        grad_decay_gate,
        grad_input_gate,
        grad_decay_rate,
        gains[3],
        *upper_grads[:2],
        upper_grads[4],
    )


def solution(mesh):
    grid = Mesh(mesh.devices.reshape(-1, 2, 2, 2, 4), ("y", "c", "xh", "xl", "z"))
    rows = P(("y", "c"), ("xl", "z", "xh"), None)
    weight = P(("xh", "xl", "z"), None)
    same = P()
    return jax.shard_map(
        body,
        mesh=grid,
        in_specs=(
            (rows, P(("y", "c")), rows)
            + (same, weight, weight, weight)
            + (same, weight, weight, weight)
            + (same, weight, weight, weight, same, same, same, same)
            + (same, weight, weight, weight)
        ),
        out_specs=(
            (rows, rows)
            + (same, weight, weight, weight)
            + (same, weight, weight, weight)
            + (same, weight, weight, weight, same, same, same, same)
            + (same, weight, weight, weight)
        ),
        check_vma=False,
    )
```

```python
import functools
import math

import jax
import jax.numpy as jnp
from jax import lax
from jax.experimental import pallas as pl
from jax.experimental.pallas import tpu as pltpu
from jax.sharding import Mesh, PartitionSpec as P

WINDOW = 1024
EPSILON = 1e-06
DECAY_SCALE = 8.0

X = ("xh", "xl")
XN = 4
F32 = jnp.float32
BF16 = jnp.bfloat16


def x_index():
    return lax.axis_index("xh") * 2 + lax.axis_index("xl")


def from_x(value, by):
    return lax.ppermute(value, X, [((i + by) % XN, i) for i in range(XN)])


def to_x(value, by):
    return lax.ppermute(value, X, [(i, (i + by) % XN) for i in range(XN)])


def flip(value, axis, by):
    return lax.ppermute(value, axis, [(i, i ^ by) for i in range(lax.axis_size(axis))])


def tie(main, *side):
    return lax.optimization_barrier((main, *side))


def after(value, *done):
    return lax.optimization_barrier((value, done))[0]


def swap(value):
    return lax.ppermute(value, "c", [(0, 1), (1, 0)])


def exchange_x(value):
    return lax.all_to_all(value, X, 0, 0)


def exchange_direct(value):
    x = x_index()
    out = jnp.zeros_like(value)
    for r in range(XN):
        piece = lax.dynamic_index_in_dim(value, (x + r) % XN, 0, keepdims=True)
        if r:
            piece = to_x(piece, r)
        out = lax.dynamic_update_slice_in_dim(out, piece, (x + XN - r) % XN, 0)
    return out


def by_core(mine, other):
    first = lax.axis_index("c") == 0
    return jnp.where(first, mine, other), jnp.where(first, other, mine)


def core_pick(zero, one):
    return jnp.where(lax.axis_index("c") == 0, zero, one)


def core_join(mine, other):
    return jnp.concatenate(by_core(mine, other), axis=-1)


def normalize(values, gain):
    return values * lax.rsqrt(jnp.mean(values * values, axis=-1, keepdims=True) + EPSILON) * gain


def smooth_gelu(values):
    return jax.nn.gelu(values, approximate=True)


def gated_unit(gate_pre, lift_pre):
    return smooth_gelu(gate_pre) * lift_pre


def branch_merge(states, branch_y):
    return states * smooth_gelu(branch_y)


def gate_terms(pre_decay, pre_admit, conv_out, decay_rate):
    retain = jax.nn.sigmoid(pre_decay)
    admit = jax.nn.sigmoid(pre_admit)
    log_decay = -DECAY_SCALE * jax.nn.softplus(decay_rate) * (0.25 + retain)
    return (jnp.exp(log_decay), jnp.sqrt(-jnp.expm1(2.0 * log_decay)) * admit * conv_out)


def matmul(left, right):
    return jnp.dot(left, right, preferred_element_type=F32)


def times_transposed(left, right):
    return lax.dot_general(left, right, (((1,), (1,)), ((), ())), preferred_element_type=F32)


def transposed_times(left, right):
    return lax.dot_general(left, right, (((0,), (0,)), ((), ())), preferred_element_type=F32)


def gather_rows(low):
    return [low] + [from_x(low, r) for r in range(1, XN)]


def chunked(low, begin, end, side=None):
    near = {1: from_x(low, 1), 3: from_x(low, 3)}
    first, later = tie(begin(0, low), low)
    far = from_x(later, 2)
    outs = [end(0, first)] + [None] * (XN - 1)
    extra = side((outs[0], near[1], near[3])) if side else None
    for k in (1, 3):
        outs[k] = end(k, begin(k, near[k]))
    far, outs[1], outs[3] = tie(far, outs[1], outs[3])
    outs[2] = end(2, begin(2, far))
    return [low, near[1], far, near[3]], outs, extra


def scatter_chunks(parts):
    total = parts[0]
    for r in (2, 1, 3):
        total = total + to_x(parts[r].astype(BF16), r).astype(F32)
    return total


def cost(microseconds):
    return pl.CostEstimate(flops=0, bytes_accessed=int(microseconds * 3.6e6), transcendentals=0)


def core_scalar():
    return lax.axis_index("c").astype(jnp.int32)[None]


def product_kernel(count, pieces, split, core_ref, *refs):
    lefts, rights = refs[:count], refs[count : 2 * count]
    mine_ref, other_ref, right = refs[2 * count :]
    rows = lefts[0].shape[0]

    @pl.when(pl.program_id(0) == 0)
    def _():
        for k in range(count):
            right[k * rows : (k + 1) * rows, :] = rights[k][...]

    left = jnp.concatenate([ref[...] for ref in lefts], axis=0)
    total = transposed_times(left, right[...]).astype(BF16)
    first = core_ref[0] == 0
    at = 0
    for low, high, width in pieces:
        zero, one = total[:, low : low + width], total[:, high : high + width]
        for ref, value in ((mine_ref, jnp.where(first, zero, one)), (other_ref, jnp.where(first, one, zero))):
            if split:
                each = ref.shape[2]
                for z in range(ref.shape[0]):
                    ref[z, 0, :, at : at + width] = value[z * each : (z + 1) * each]
            else:
                ref[:, at : at + width] = value
        at += width


def chunk_product(lefts, rights, pieces, split):
    rows, deep = lefts[0].shape
    width = rights[0].shape[1]
    count = len(lefts)
    kept = sum(piece[2] for piece in pieces)
    if split:
        tile = deep // XN
        shape = (4, XN, tile // 4, kept)
        spec = pl.BlockSpec((4, 1, tile // 4, kept), lambda i: (0, i, 0, 0))
    else:
        tile = next((t for t in (384, 256, 128) if deep % t == 0), deep)
        shape = (deep, kept)
        spec = pl.BlockSpec((tile, kept), lambda i: (i, 0))
    mine, other = pl.pallas_call(
        functools.partial(product_kernel, count, pieces, split),
        grid=(deep // tile,),
        in_specs=[pl.BlockSpec(memory_space=pltpu.SMEM)]
        + [pl.BlockSpec((rows, tile), lambda i: (0, i)) for _ in lefts]
        + [pl.BlockSpec((rows, width), lambda i: (0, 0)) for _ in rights],
        out_specs=[spec, spec],
        out_shape=[jax.ShapeDtypeStruct(shape, BF16)] * 2,
        scratch_shapes=[pltpu.VMEM((count * rows, width), BF16)],
        compiler_params=pltpu.CompilerParams(vmem_limit_bytes=48 << 20),
        cost_estimate=pl.CostEstimate(
            flops=2 * count * rows * deep * width,
            bytes_accessed=2 * (count * rows * (deep + width) + 2 * deep * kept),
            transcendentals=0,
        ),
    )(core_scalar(), *lefts, *rights)
    total = (mine.astype(F32) + swap(other).astype(F32)).astype(BF16)
    return total.reshape(-1, kept)


def unit_pieces(quarter):
    wide = quarter * 5 // 9
    return ((0, quarter - wide, wide), (quarter, 2 * quarter - wide, wide))


def half_pieces(width):
    half = width // 4
    return ((0, half, half), (2 * half, 3 * half, half))


def row_pieces(width):
    return ((0, width // 2, width // 2),)


def kv_places(rows):
    places = []
    for x in range(XN):
        for z in range(4):
            for j in range(2):
                position = (j * 4 + z) * 2 + x // 2
                places.append((x * 4 + z, j, x % 2, WINDOW + position * rows))
    return places


def attend_scores(pos_ref, q_ref, key_s, scale):
    rows, size = q_ref.shape[1], key_s.shape[1]
    heads = q_ref.shape[2] // size
    start = pl.multiple_of(pos_ref[pl.program_id(0)] * rows, rows)
    query = q_ref[0]
    query = jnp.concatenate([query[:, h * size : (h + 1) * size] for h in range(heads)], axis=0)
    key = key_s[pl.ds(start, WINDOW + rows), :]
    scores = times_transposed(query, key) * scale
    row = lax.broadcasted_iota(jnp.int32, scores.shape, 0) % rows
    col = lax.broadcasted_iota(jnp.int32, scores.shape, 1)
    allowed = (col > row) & (col <= row + WINDOW) & (col >= WINDOW - start)
    return start, query, key, jnp.where(allowed, scores, -1e30)


def load_kv(kv_ref, key_s, value_s):
    rows = kv_ref.shape[2]
    key_s[:WINDOW, :] = jnp.zeros((WINDOW, key_s.shape[1]), key_s.dtype)
    value_s[:WINDOW, :] = jnp.zeros((WINDOW, key_s.shape[1]), key_s.dtype)
    for source, j, kind, first in kv_places(rows):
        (value_s if kind else key_s)[first : first + rows, :] = kv_ref[source, j]


def attend_forward_kernel(scale, pos_ref, q_ref, kv_ref, out_ref, lse_ref, key_s, value_s):
    rows, size = q_ref.shape[1], key_s.shape[1]

    @pl.when(pl.program_id(0) == 0)
    def _():
        load_kv(kv_ref, key_s, value_s)

    start, query, key, scores = attend_scores(pos_ref, q_ref, key_s, scale)
    highest = jnp.max(scores, axis=-1, keepdims=True)
    lse = highest + jnp.log(jnp.sum(jnp.exp(scores - highest), axis=-1, keepdims=True))
    probs = jnp.exp(scores - lse).astype(BF16)
    mixed = matmul(probs, value_s[pl.ds(start, WINDOW + rows), :]).astype(BF16)
    out_ref[0] = jnp.concatenate(
        [mixed[h * rows : (h + 1) * rows] for h in range(q_ref.shape[2] // size)], axis=1
    )
    lse_ref[0] = lse


def attend_backward_kernel(
    scale, pos_ref, q_ref, kv_ref, grad_ref, lse_ref, dq_ref, dkv_ref, key_s, value_s, dk_s, dv_s
):
    rows, size = q_ref.shape[1], key_s.shape[1]
    heads = q_ref.shape[2] // size

    @pl.when(pl.program_id(0) == 0)
    def _():
        load_kv(kv_ref, key_s, value_s)
        dk_s[...] = jnp.zeros_like(dk_s)
        dv_s[...] = jnp.zeros_like(dv_s)

    start, query, key, scores = attend_scores(pos_ref, q_ref, key_s, scale)
    span = pl.ds(start, WINDOW + rows)
    probs = jnp.exp(scores - lse_ref[0])
    grad = grad_ref[0]
    grad = jnp.concatenate([grad[:, h * size : (h + 1) * size] for h in range(heads)], axis=0)
    prob_grad = times_transposed(grad, value_s[span, :])
    delta = jnp.sum(probs * prob_grad, axis=-1, keepdims=True)
    score_grad = (probs * (prob_grad - delta)).astype(BF16)
    query_grad = (matmul(score_grad, key) * scale).astype(BF16)
    dq_ref[0] = jnp.concatenate(
        [query_grad[h * rows : (h + 1) * rows] for h in range(heads)], axis=1
    )
    dk_s[span, :] += transposed_times(score_grad, query) * scale
    dv_s[span, :] += transposed_times(probs.astype(BF16), grad)

    @pl.when(pl.program_id(0) == pl.num_programs(0) - 1)
    def _():
        for source, j, kind, first in kv_places(rows):
            dkv_ref[source, j] = (dv_s if kind else dk_s)[first : first + rows, :].astype(BF16)


def whole(array):
    return pl.BlockSpec(array.shape, lambda r: (0,) * len(array.shape))


def by_block(*shape):
    return pl.BlockSpec((1,) + shape, lambda r: (r, 0, 0))


def kv_scratch(kv, dtype):
    return pltpu.VMEM((WINDOW + 16 * kv.shape[2], kv.shape[3]), dtype)


def attend_forward(positions, query, kv):
    blocks, rows, width = query.shape
    size = kv.shape[3]
    stacked = rows * (width // size)
    return pl.pallas_call(
        functools.partial(attend_forward_kernel, size**-0.5),
        grid=(blocks,),
        in_specs=[pl.BlockSpec(memory_space=pltpu.SMEM), by_block(rows, width), whole(kv)],
        out_specs=[by_block(rows, width), by_block(stacked, 1)],
        out_shape=[
            jax.ShapeDtypeStruct(query.shape, BF16),
            jax.ShapeDtypeStruct((blocks, stacked, 1), F32),
        ],
        scratch_shapes=[kv_scratch(kv, BF16), kv_scratch(kv, BF16)],
        cost_estimate=cost(7),
        compiler_params=pltpu.CompilerParams(vmem_limit_bytes=40 << 20),
    )(positions, query, kv)


def attend_backward(positions, query, kv, grad, lse):
    blocks, rows, width = query.shape
    size = kv.shape[3]
    stacked = rows * (width // size)
    return pl.pallas_call(
        functools.partial(attend_backward_kernel, size**-0.5),
        grid=(blocks,),
        in_specs=[
            pl.BlockSpec(memory_space=pltpu.SMEM),
            by_block(rows, width),
            whole(kv),
            by_block(rows, width),
            by_block(stacked, 1),
        ],
        out_specs=[by_block(rows, width), whole(kv)],
        out_shape=[
            jax.ShapeDtypeStruct(query.shape, BF16),
            jax.ShapeDtypeStruct(kv.shape, BF16),
        ],
        scratch_shapes=[
            kv_scratch(kv, BF16),
            kv_scratch(kv, BF16),
            kv_scratch(kv, F32),
            kv_scratch(kv, F32),
        ],
        cost_estimate=cost(9),
        compiler_params=pltpu.CompilerParams(vmem_limit_bytes=40 << 20),
    )(positions, query, kv, grad, lse)


def scan_kernel(backward, factor_ref, update_ref, state_ref):
    tiles = factor_ref.shape[0] // 8
    width = factor_ref.shape[1]
    row = lax.broadcasted_iota(jnp.int32, (8, width), 0)

    def turn(index, carry):
        tile = tiles - 1 - index if backward else index
        span = pl.ds(pl.multiple_of(tile * 8, 8), 8)
        factor, update = factor_ref[span, :], update_ref[span, :]
        for reach in (1, 2, 4):
            shift = 8 - reach if backward else reach
            inside = row < 8 - reach if backward else row >= reach
            far_update = pltpu.roll(update, shift, 0)
            far_factor = pltpu.roll(factor, shift, 0)
            update = jnp.where(inside, factor * far_update + update, update)
            factor = jnp.where(inside, factor * far_factor, factor)
        state = factor * carry + update
        state_ref[span, :] = state
        last = state[0:1] if backward else state[7:8]
        return jnp.broadcast_to(last, (8, width))

    lax.fori_loop(0, tiles, turn, jnp.zeros((8, width), F32), unroll=8)


def linear_scan(factors, updates, backward):
    return pl.pallas_call(
        functools.partial(scan_kernel, backward),
        out_shape=jax.ShapeDtypeStruct(factors.shape, F32),
        cost_estimate=cost(1.5),
        compiler_params=pltpu.CompilerParams(vmem_limit_bytes=24 << 20),
    )(factors, updates)


def to_sequence(chunks):
    rows, width = chunks[0].shape[0], chunks[0].shape[1] // 4
    sent = jnp.stack(
        [jnp.stack([part[:, b * width : (b + 1) * width] for part in chunks]) for b in range(4)]
    )
    got = lax.all_to_all(sent, "z", 0, 0)
    got = jnp.roll(got, x_index(), axis=1).reshape(4, 2, 2, rows, width)
    return got.transpose(2, 0, 1, 3, 4).reshape(16 * rows, width)


def from_sequence(values):
    rows, width = values.shape[0] // 16, values.shape[1]
    sent = values.reshape(2, 4, 2, rows, width).transpose(1, 2, 0, 3, 4)
    sent = jnp.roll(sent.reshape(4, XN, rows, width), -x_index(), axis=1)
    got = lax.all_to_all(sent, "z", 0, 0)
    return [jnp.concatenate([got[b, k] for b in range(4)], axis=1) for k in range(XN)]


def shift_down(values, by):
    if by == 0:
        return values
    return jnp.concatenate([jnp.zeros_like(values[:by]), values[:-by]], axis=0)


def shift_up(values, by):
    if by == 0:
        return values
    return jnp.concatenate([values[by:], jnp.zeros_like(values[:by])], axis=0)


def unit_slices(weight):
    quarter = weight.shape[1] // XN
    wide = quarter * 5 // 9
    skip = quarter - wide
    keep = lax.broadcasted_iota(jnp.int32, (weight.shape[0], wide), 1) >= wide - skip
    picked = []
    for member in range(XN):
        columns = weight[:, member * quarter : (member + 1) * quarter]
        picked.append(core_pick(columns[:, :wide], jnp.where(keep, columns[:, skip:], 0)))
    return jnp.stack(picked)


def half_slices(weight):
    quarter = weight.shape[1] // XN
    half = quarter // 2
    picked = []
    for member in range(XN):
        columns = weight[:, member * quarter : (member + 1) * quarter]
        picked.append(core_pick(columns[:, :half], columns[:, half:]))
    return jnp.stack(picked)


def own_half(weight):
    half = weight.shape[-1] // 2
    return core_pick(weight[..., :half], weight[..., half:])


def other_half(weight):
    half = weight.shape[-1] // 2
    return core_pick(weight[..., half:], weight[..., :half])


def gather_direct(value):
    z = lax.axis_index("z")
    out = jnp.zeros((value.shape[0], 4) + value.shape[1:], value.dtype)
    for by in range(4):
        piece = flip(value, "z", by) if by else value
        out = lax.dynamic_update_slice_in_dim(out, piece[:, None], z ^ by, 1)
    return out


def row_join(rows):
    return core_join(rows, swap(rows))


def join_kernel(plans, core_ref, mine_ref, other_ref, *outs):
    first = core_ref[0] == 0
    each = mine_ref.shape[2]
    for z in range(mine_ref.shape[0]):
        mine, other = mine_ref[z, 0], other_ref[z, 0]
        zero, one = jnp.where(first, mine, other), jnp.where(first, other, mine)
        for out, pieces in zip(outs, plans):
            at = 0
            for core, low, high in pieces:
                out[z * each : (z + 1) * each, at : at + high - low] = (one if core else zero)[:, low:high]
                at += high - low


def column_join(columns, plans):
    zs, xs, rows, width = columns.shape
    spec = pl.BlockSpec((zs, 1, rows, width), lambda i: (0, i, 0, 0))
    widths = [sum(high - low for _, low, high in pieces) for pieces in plans]
    return pl.pallas_call(
        functools.partial(join_kernel, plans),
        grid=(xs,),
        in_specs=[pl.BlockSpec(memory_space=pltpu.SMEM), spec, spec],
        out_specs=[pl.BlockSpec((zs * rows, out), lambda i: (i, 0)) for out in widths],
        out_shape=[jax.ShapeDtypeStruct((zs * xs * rows, out), BF16) for out in widths],
        cost_estimate=cost(6),
        compiler_params=pltpu.CompilerParams(vmem_limit_bytes=40 << 20),
    )(core_scalar(), columns, swap(columns))


def unit_plan(unit_width):
    wide = unit_width // 2
    skip = wide * 4 // 5
    return (
        (0, 0, wide),
        (1, wide - skip, wide),
        (0, wide, 2 * wide),
        (1, 2 * wide - skip, 2 * wide),
    )


def half_plan(first, width):
    half = width // 2
    return tuple(
        (core, first + side * half, first + (side + 1) * half) for side in range(2) for core in range(2)
    )


def reduce_z(grad):
    return lax.psum_scatter(grad, "z", scatter_dimension=0, tiled=True)


def reduce_direct(grad, axis):
    at = lax.axis_index(axis)
    parts = grad.reshape(4, -1, grad.shape[1])
    total = lax.dynamic_index_in_dim(parts, at, 0, keepdims=False).astype(F32)
    for by in (2, 1, 3):
        piece = lax.dynamic_index_in_dim(parts, at ^ by, 0, keepdims=False)
        total = total + flip(piece, axis, by).astype(F32)
    return total.astype(BF16)


def units_of(columns, rows):
    own = columns[0].shape[0] // XN
    unit = functools.reduce(math.gcd, [own] + [array.shape[0] for array in rows])
    half = rows[0].shape[1]
    chunk = functools.reduce(math.gcd, [half] + [array.shape[1] // 2 for array in columns])
    column_units = [
        (a, lane, part)
        for a, array in enumerate(columns)
        for lane in range(array.shape[1] // chunk)
        for part in range(own // unit)
    ]
    row_units = [
        (a, part, lane)
        for a, array in enumerate(rows)
        for part in range(array.shape[0] // unit)
        for lane in range(half // chunk)
    ]
    column_slots, row_slots = -(-len(column_units) // 4), -(-len(row_units) // 4)
    return unit, chunk, own, column_units, row_units, column_slots, row_slots


def pack_kernel(plan, column_count, *refs):
    unit, chunk, own, column_units, row_units, column_slots, row_slots = plan
    columns, rows, out = refs[:column_count], refs[column_count:-1], refs[-1]
    slots = XN * column_slots + row_slots
    for n, (a, lane, part) in enumerate(column_units):
        for x in range(XN):
            first = ((n % 4) * slots + x * column_slots + n // 4) * unit
            out[first : first + unit, :] = columns[a][
                x * own + part * unit : x * own + (part + 1) * unit,
                lane * chunk : (lane + 1) * chunk,
            ]
    for n, (a, part, lane) in enumerate(row_units):
        first = ((n % 4) * slots + XN * column_slots + n // 4) * unit
        out[first : first + unit, :] = rows[a][
            part * unit : (part + 1) * unit, lane * chunk : (lane + 1) * chunk
        ]
    empty = jnp.zeros((unit, chunk), BF16)
    for n in range(len(column_units), 4 * column_slots):
        for x in range(XN):
            first = ((n % 4) * slots + x * column_slots + n // 4) * unit
            out[first : first + unit, :] = empty
    for n in range(len(row_units), 4 * row_slots):
        first = ((n % 4) * slots + XN * column_slots + n // 4) * unit
        out[first : first + unit, :] = empty


def unpack_kernel(plan, kinds, packed, *outs):
    unit, chunk, own, column_units, row_units, column_slots, row_slots = plan
    slots = XN * column_slots + row_slots

    def block(n, c, slot):
        first = (((n % 4) * 2 + c) * slots + slot + n // 4) * unit
        return packed[first : first + unit, :].astype(F32)

    for n, (a, lane, part) in enumerate(column_units):
        kind, width, first_out = kinds[a]
        rows = slice(part * unit, (part + 1) * unit)
        for c in range(2):
            got = [block(n, c, x * column_slots) for x in range(XN)]
            if kind == "attend":
                at = c * width + lane * chunk
                query = 2 * width * 3 // 4
                for x in range(XN):
                    if at < query:
                        to = x * query + at
                        outs[first_out][rows, to : to + chunk] = got[x]
                if at >= query:
                    size = 2 * width - query
                    to = at - query
                    outs[first_out + 1][rows, to : to + chunk] = got[0] + got[2]
                    outs[first_out + 1][rows, size + to : size + to + chunk] = got[1] + got[3]
                continue
            each = width // 2
            which, at = divmod(lane * chunk, each)
            if kind == "unit":
                skip = each * 4 // 5
                quarter = each + skip
                at = at + c * skip
                if c == 1 and at < each:
                    continue
            else:
                quarter = 2 * each
                at = at + c * each
            for x in range(XN):
                to = x * quarter + at
                outs[first_out + which][rows, to : to + chunk] = got[x]
    row_outs = outs[-(1 + max(a for a, _, _ in row_units)) :]
    half = row_outs[0].shape[1] // 2
    for n, (a, part, lane) in enumerate(row_units):
        for c in range(2):
            to = c * half + lane * chunk
            row_outs[a][part * unit : (part + 1) * unit, to : to + chunk] = block(
                n, c, XN * column_slots
            )


def pack(columns, rows):
    plan = units_of(columns, rows)
    unit, chunk, _, _, _, column_slots, row_slots = plan
    return pl.pallas_call(
        functools.partial(pack_kernel, plan, len(columns)),
        out_shape=jax.ShapeDtypeStruct(
            (4 * (XN * column_slots + row_slots) * unit, chunk), BF16
        ),
        cost_estimate=cost(2),
        compiler_params=pltpu.CompilerParams(vmem_limit_bytes=40 << 20),
    )(*columns, *rows), plan


def to_owners(part, plan):
    unit, chunk, _, _, _, column_slots, row_slots = plan
    split = XN * column_slots * unit
    columns = exchange_x(part[:split].reshape(XN, column_slots * unit, chunk))
    return jnp.concatenate([columns.reshape(split, chunk), part[split:]], axis=0)


def spread(part):
    return lax.all_gather(part, ("y", "c"), axis=0, tiled=True)


def spread_direct(part):
    y = lax.axis_index("y")
    out = jnp.zeros((4,) + part.shape, part.dtype)
    for by in range(4):
        piece = flip(part, "y", by) if by else part
        out = lax.dynamic_update_slice_in_dim(out, piece[None], y ^ by, 0)
    return jnp.stack(by_core(out, swap(out)), axis=1).reshape(-1, part.shape[1])


def unpack(packed, plan, kinds, shapes):
    return pl.pallas_call(
        functools.partial(unpack_kernel, plan, kinds),
        out_shape=[jax.ShapeDtypeStruct(shape, F32) for shape in shapes],
        cost_estimate=cost(4),
        compiler_params=pltpu.CompilerParams(vmem_limit_bytes=48 << 20),
    )(packed)


def butterfly(value, axes):
    for axis in axes:
        by = 1
        while by < lax.axis_size(axis):
            value = value + flip(value, axis, by)
            by *= 2
    return value


def dense_forward(residual, gain, unit_weight, drop_weight):
    normed, norm_pull = jax.vjp(normalize, residual, gain)
    wide = unit_weight.shape[1] // 2
    kept = [None] * XN

    def begin(k, rows):
        return matmul(rows, unit_weight)

    def end(k, pre):
        hidden, unit_pull = jax.vjp(gated_unit, pre[:, :wide], pre[:, wide:])
        kept[k] = (hidden.astype(BF16), unit_pull)
        return matmul(kept[k][0], drop_weight)

    chunks, parts, _ = chunked(normed.astype(BF16), begin, end)
    return parts, (norm_pull, chunks, kept)


def dense_backward(residual_grad, stored, unit_weight, drop_weight, grad_chunks=None, side=None):
    norm_pull, chunks, kept = stored
    pre_grads = [None] * XN

    def begin(k, rows):
        return times_transposed(rows, drop_weight)

    def end(k, hidden_grad):
        pre_grad = kept[k][1](hidden_grad)
        pre_grads[k] = jnp.concatenate([part.astype(BF16) for part in pre_grad], axis=1)
        return times_transposed(pre_grads[k], unit_weight)

    extra = None
    if grad_chunks is None:
        grad_chunks, parts, extra = chunked(residual_grad.astype(BF16), begin, end, side)
    else:
        parts = [None] * XN
        for k in (0, 1, 3, 2):
            parts[k] = end(k, begin(k, grad_chunks[k]))
    input_grad, gain_grad = norm_pull(scatter_chunks(parts))

    def products(done):
        pre, grads = after((pre_grads, grad_chunks), done)
        return (
            chunk_product(chunks, pre, unit_pieces(unit_weight.shape[1] // 2), True),
            chunk_product(
                [hidden for hidden, _ in kept], grads, row_pieces(drop_weight.shape[1]), False
            ),
        )

    return residual_grad + input_grad, gain_grad, products, extra


def body(
    tokens,
    lengths,
    cotangent,
    attend_gain,
    query_weight,
    keyval_weight,
    attend_output,
    lower_gain,
    lower_gate,
    lower_lift,
    lower_drop,
    recur_gain,
    recur_input,
    recur_branch,
    recur_output,
    temporal_kernel,
    decay_gate,
    input_gate,
    decay_rate,
    upper_gain,
    upper_gate,
    upper_lift,
    upper_drop,
):
    x, z = x_index(), lax.axis_index("z")
    row_count, features = tokens.shape[1:]
    size = keyval_weight.shape[1] // 2
    query_width = query_weight.shape[1] // XN
    drop_rows, recur_rows = lower_drop.shape[0], recur_output.shape[0]
    channels = 4 * recur_rows
    tap_count = temporal_kernel.shape[0]
    even = x % 2 == 0
    members = (x + jnp.arange(XN, dtype=jnp.int32)) % XN
    positions = ((members % 2 * 4 + z) * 2 + members // 2).astype(jnp.int32)
    token_pos = positions[0] * row_count + jnp.arange(row_count, dtype=jnp.int32)
    valid = (token_pos < lengths[0]).astype(F32)[:, None]

    start_rows = tokens[0].astype(F32)
    normed_attend, attend_pull = jax.vjp(normalize, start_rows, attend_gain)
    member_query = query_weight.reshape(-1, XN, query_width).transpose(1, 0, 2)
    member_kv = jnp.stack([keyval_weight[:, (m % 2) * size : (m % 2 + 1) * size] for m in range(XN)])
    lower_columns = exchange_x(
        jnp.concatenate([unit_slices(lower_gate), unit_slices(lower_lift)], axis=2)
    )
    unit_width = lower_columns.shape[2]
    attend_columns = own_half(jnp.concatenate([member_query, member_kv], axis=2))
    half_in = lax.all_to_all(jnp.repeat(attend_columns, 4, axis=0), X + ("z",), 0, 0)
    attend_in = row_join(half_in.reshape(features, -1))
    half_out = gather_direct(own_half(attend_output)[None])
    lower_rows = lax.all_gather(own_half(lower_drop), "z", axis=0, tiled=True)

    attend_rows = jnp.concatenate(gather_rows(normed_attend.astype(BF16)), axis=0)
    attend_rows, attend_in, lower_columns, lower_rows = tie(
        attend_rows, attend_in, lower_columns, lower_rows
    )
    lower_columns = lax.all_gather(lower_columns, "z", axis=0)
    recur_input, recur_branch, upper_gate, upper_lift = after(
        (recur_input, recur_branch, upper_gate, upper_lift), attend_rows
    )
    upper_columns = exchange_direct(
        jnp.concatenate(
            [
                half_slices(recur_input),
                half_slices(recur_branch),
                unit_slices(upper_gate),
                unit_slices(upper_lift),
            ],
            axis=2,
        )
    )
    mixed_in = matmul(attend_rows, attend_in).astype(BF16).reshape(XN, row_count, -1)
    queries = mixed_in[:, :, :query_width]
    kv_part = mixed_in[:, :, query_width:]
    kv_send = jnp.stack(
        [jnp.where(even, kv_part[0], kv_part[3]), jnp.where(even, kv_part[1], kv_part[0])]
    )
    kv = lax.all_to_all(
        jnp.broadcast_to(kv_send[None], (16,) + kv_send.shape), X + ("z",), 0, 0
    )
    out_grad = cotangent[0].astype(F32) * valid
    out_grad_chunks = gather_rows(after(out_grad.astype(BF16), kv))
    kv, half_out = tie(kv, half_out)
    attend_out = row_join(half_out.reshape(query_width, -1))
    attended, log_total = attend_forward(positions, queries, kv)
    attended, out_grad_chunks = tie(attended, out_grad_chunks)
    attend_back = attended.reshape(XN * row_count, query_width)
    parts = [matmul(attended[k], attend_out) for k in range(XN)]
    first_rows = start_rows + scatter_chunks(parts)
    first_rows, upper_columns = tie(first_rows, upper_columns)

    lower_columns, lower_rows = after((lower_columns, lower_rows), first_rows)
    (lower_unit,) = column_join(lower_columns, (unit_plan(unit_width),))
    lower_down = row_join(lower_rows)
    recur_columns = lax.all_gather(upper_columns[:, :, :channels], "z", axis=0)
    upper_rows = own_half(jnp.concatenate([recur_output, upper_drop], axis=0))
    upper_rows = lax.all_gather(after(upper_rows, parts), "z", axis=0)
    upper_columns = lax.all_gather(after(upper_columns, parts)[:, :, channels:], "z", axis=0)

    parts, lower_kept = dense_forward(first_rows, lower_gain, lower_unit, lower_down)
    second_rows = first_rows + scatter_chunks(parts)
    recur_columns, upper_rows = after((recur_columns, upper_rows), second_rows)
    (recur_in,) = column_join(recur_columns, (half_plan(0, channels),))
    recur_out = row_join(upper_rows[:, :recur_rows].reshape(4 * recur_rows, -1))

    normed_recur, recur_pull = jax.vjp(normalize, second_rows, recur_gain)
    recur_chunks, branches, _ = chunked(
        normed_recur.astype(BF16), lambda k, rows: matmul(rows, recur_in), lambda k, branch: branch
    )
    branch_y = [part[:, channels:] for part in branches]
    x_seq = to_sequence([part[:, :channels].astype(BF16) for part in branches]).astype(F32)
    upper_columns, upper_rows = after((upper_columns, upper_rows), branches)
    (upper_unit,) = column_join(upper_columns, (unit_plan(unit_width),))
    upper_down = row_join(upper_rows[:, recur_rows:].reshape(4 * drop_rows, -1))
    block = x * 4 + z
    width = decay_gate.shape[1]
    own_decay = lax.dynamic_slice_in_dim(decay_rate, block * width, width, 0)
    own_taps = lax.dynamic_slice_in_dim(temporal_kernel, block * width, width, 1)
    own_decay_gate = lax.dynamic_index_in_dim(decay_gate, block, 0, keepdims=False)
    own_input_gate = lax.dynamic_index_in_dim(input_gate, block, 0, keepdims=False)
    shifted = [shift_down(x_seq, k) for k in range(tap_count)]
    conv_out = sum(own_taps[k] * shifted[k] for k in range(tap_count))
    conv_low = conv_out.astype(BF16)
    pre_decay = matmul(conv_low, own_decay_gate)
    pre_admit = matmul(conv_low, own_input_gate)
    (factors, updates), gate_pull = jax.vjp(gate_terms, pre_decay, pre_admit, conv_out, own_decay)
    states = linear_scan(factors, updates, False)
    states_back = from_sequence(states.astype(BF16))
    merge_pulls, merged_low, parts = [], [], []
    for part, y_part in zip(states_back, branch_y):
        merged, merge_pull = jax.vjp(branch_merge, part.astype(F32), y_part)
        merge_pulls.append(merge_pull)
        merged_low.append(merged.astype(BF16))
        parts.append(matmul(merged_low[-1], recur_out))
    third_rows = second_rows + scatter_chunks(parts)

    out_parts, upper_kept = dense_forward(third_rows, upper_gain, upper_unit, upper_down)

    residual_grad, grad_upper_gain, upper_products, _ = dense_backward(
        out_grad, upper_kept, upper_unit, upper_down, out_grad_chunks
    )
    recur_grad_chunks, merged_grads, upper_grads = chunked(
        residual_grad.astype(BF16),
        lambda k, rows: times_transposed(rows, recur_out),
        lambda k, merged_grad: merge_pulls[k](merged_grad),
        upper_products,
    )
    fourth_rows = third_rows + scatter_chunks(after(out_parts, merged_grads))
    out_tokens = (fourth_rows * valid).astype(BF16)[None]
    state_grad = to_sequence([part[0].astype(BF16) for part in merged_grads]).astype(F32)
    adjoint = linear_scan(shift_up(factors, 1), state_grad, True)
    decay_grad, admit_grad, conv_grad, own_decay_grad = gate_pull(
        (adjoint * shift_down(states, 1), adjoint)
    )
    decay_grad_low, admit_grad_low = decay_grad.astype(BF16), admit_grad.astype(BF16)
    conv_grad = (
        conv_grad
        + times_transposed(decay_grad_low, own_decay_gate)
        + times_transposed(admit_grad_low, own_input_gate)
    )
    own_gate_grad = transposed_times(conv_low, decay_grad_low)
    own_admit_grad = transposed_times(conv_low, admit_grad_low)
    tap_grads = jnp.stack([jnp.sum(conv_grad * shifted[k], axis=0) for k in range(tap_count)])
    x_seq_grad = sum(own_taps[k] * shift_up(conv_grad, k) for k in range(tap_count))
    channel_grads = jnp.concatenate(
        [
            own_gate_grad,
            own_admit_grad,
            tap_grads,
            own_decay_grad[None],
            jnp.zeros((3, width), F32),
        ],
        axis=0,
    )
    branch_x_grad = from_sequence(x_seq_grad.astype(BF16))
    branch_x_grad, out_tokens = tie(branch_x_grad, out_tokens)
    branch_grad = [
        jnp.concatenate([x_part, part[1].astype(BF16)], axis=1)
        for x_part, part in zip(branch_x_grad, merged_grads)
    ]
    normed_grad = scatter_chunks([times_transposed(part, recur_in) for part in branch_grad])
    recur_input_grad, grad_recur_gain = recur_pull(normed_grad)
    residual_grad = residual_grad + recur_input_grad
    residual_grad, upper_grads = tie(residual_grad, upper_grads)
    upper_unit_grad, upper_drop_grad = (reduce_z(grad) for grad in upper_grads)

    def recur_products(done):
        branch, grads = after((branch_grad, recur_grad_chunks), done)
        return (
            chunk_product(recur_chunks, branch, half_pieces(2 * channels), True),
            chunk_product(merged_low, grads, row_pieces(features), False),
        )

    residual_grad, grad_lower_gain, lower_products, recur_grads = dense_backward(
        residual_grad, lower_kept, lower_unit, lower_down, None, recur_products
    )
    residual_grad, recur_grads, upper_drop_grad = tie(
        residual_grad, recur_grads, upper_drop_grad
    )
    recur_in_grad, recur_out_grad = (reduce_z(grad) for grad in recur_grads)
    grad_chunks, attend_grad, lower_grads = chunked(
        residual_grad.astype(BF16),
        lambda k, rows: times_transposed(rows, attend_out).astype(BF16),
        lambda k, grad: grad,
        lambda done: lower_products((done, upper_unit_grad)),
    )
    attend_grad = jnp.stack(attend_grad)
    query_grad, kv_grad = attend_backward(
        positions, queries, kv, attend_grad, log_total
    )
    kv_grad = lax.all_to_all(kv_grad, X + ("z",), 0, 0)
    out_grad = chunk_product(
        [attended[k] for k in range(XN)], grad_chunks, row_pieces(features), False
    )
    kv_grad, query_grad, out_grad, lower_grads = tie(kv_grad, query_grad, out_grad, lower_grads)
    lower_unit_grad, lower_drop_grad = (reduce_z(grad) for grad in lower_grads)
    kv_grad = jnp.sum(kv_grad.astype(F32), axis=0).astype(BF16)
    nothing = jnp.zeros_like(kv_grad[0])
    kv_grad = jnp.stack(
        [
            jnp.where(even, kv_grad[0], kv_grad[1]),
            jnp.where(even, kv_grad[1], nothing),
            nothing,
            jnp.where(even, nothing, kv_grad[0]),
        ]
    )
    mixed_grad = jnp.concatenate([query_grad, kv_grad], axis=2).reshape(XN * row_count, -1)
    mixed_chunks = [mixed_grad[k * row_count : (k + 1) * row_count] for k in range(XN)]
    attend_chunks = [attend_rows[k * row_count : (k + 1) * row_count] for k in range(XN)]
    in_grad = chunk_product(attend_chunks, mixed_chunks, row_pieces(mixed_grad.shape[1]), True)
    lanes = in_grad.shape[1]
    out_rows = out_grad.reshape(4, -1, features // 2)
    both = [in_grad.reshape(4, -1, lanes)]
    both += [out_rows[:, :, at : at + lanes] for at in range(0, features // 2, lanes)]
    both = reduce_direct(jnp.concatenate(both, axis=1).reshape(-1, lanes), "z")
    normed_grad = scatter_chunks(
        [times_transposed(part, attend_in) for part in after(mixed_chunks, in_grad)]
    )
    channel_grads = butterfly(after(channel_grads, kv_grad), ("c", "y"))
    both, normed_grad, channel_grads = tie(both, normed_grad, channel_grads)
    recur_in_grad, recur_out_grad = after((recur_in_grad, recur_out_grad), both)
    packed, upper_plan = pack([upper_unit_grad, recur_in_grad], [upper_drop_grad, recur_out_grad])
    channel_grads = lax.all_to_all(
        jnp.broadcast_to(channel_grads, (16,) + channel_grads.shape), X + ("z",), 0, 0
    )
    packed, channel_grads = tie(reduce_direct(packed, "y"), channel_grads)
    upper_packed = spread(to_owners(packed, upper_plan))
    in_grad, out_grad = both[: features // 4], both[features // 4 :].reshape(-1, features // 16, lanes)
    out_grad = jnp.concatenate([out_grad[k] for k in range(out_grad.shape[0])], axis=1)
    packed, lower_plan = pack([lower_unit_grad, in_grad], [lower_drop_grad, out_grad])
    packed, upper_packed = tie(reduce_direct(packed, "y"), upper_packed)
    lower_packed = spread(to_owners(packed, lower_plan))
    attend_input_grad, grad_attend_gain = attend_pull(normed_grad)
    gains = butterfly(
        jnp.stack([grad_attend_gain, grad_lower_gain, grad_recur_gain, grad_upper_gain]),
        ("c", "xl", "xh", "z", "y"),
    )
    residual_grad = residual_grad + attend_input_grad
    grad_decay_gate = channel_grads[:, :width]
    grad_input_gate = channel_grads[:, width : 2 * width]
    grad_temporal_kernel = (
        channel_grads[:, 2 * width : 2 * width + tap_count]
        .transpose(1, 0, 2)
        .reshape(tap_count, -1)
    )
    grad_decay_rate = channel_grads[:, 2 * width + tap_count].reshape(-1)
    upper_grads = unpack(
        upper_packed,
        upper_plan,
        (("unit", unit_width, 0), ("half", channels, 2)),
        [a.shape for a in (upper_gate, upper_lift, recur_input, recur_branch, upper_drop, recur_output)],
    )
    lower_grads = unpack(
        lower_packed,
        lower_plan,
        (("unit", unit_width, 0), ("attend", in_grad.shape[1], 2)),
        [a.shape for a in (lower_gate, lower_lift, query_weight, keyval_weight, lower_drop, attend_output)],
    )
    return (
        out_tokens,
        residual_grad[None],
        gains[0],
        *lower_grads[2:4],
        lower_grads[5],
        gains[1],
        *lower_grads[:2],
        lower_grads[4],
        gains[2],
        *upper_grads[2:4],
        upper_grads[5],
        grad_temporal_kernel,
        grad_decay_gate,
        grad_input_gate,
        grad_decay_rate,
        gains[3],
        *upper_grads[:2],
        upper_grads[4],
    )


def solution(mesh):
    grid = Mesh(mesh.devices.reshape(-1, 2, 2, 2, 4), ("y", "c", "xh", "xl", "z"))
    rows = P(("y", "c"), ("xl", "z", "xh"), None)
    weight = P(("xh", "xl", "z"), None)
    same = P()
    return jax.shard_map(
        body,
        mesh=grid,
        in_specs=(
            (rows, P(("y", "c")), rows)
            + (same, weight, weight, weight)
            + (same, weight, weight, weight)
            + (same, weight, weight, weight, same, same, same, same)
            + (same, weight, weight, weight)
        ),
        out_specs=(
            (rows, rows)
            + (same, weight, weight, weight)
            + (same, weight, weight, weight)
            + (same, weight, weight, weight, same, same, same, same)
            + (same, weight, weight, weight)
        ),
        check_vma=False,
    )
```
